256 devices in a mesh: row: 32 (over x, z), col: 8 (over y, core).
Axes of the slice: x: 4, y: 4, z: 8, core: 2. Of those that a mesh axis runs over, the one named last changes fastest.
Arguments:
- panel: float32 [32768, 256], P('row', 'col'), as said below
- trailing: bfloat16 [32768, 16384], P('row', 'col'), may hold values from -6 to 6
Outputs:
- r_factor: float32 [256, 256], replicated
- top_rows: float32 [256, 16384], P(None, 'col')
- updated: bfloat16 [32768, 16384], P('row', 'col')
The draws below stay inside these ranges and needn't reach their ends.
Inputs may be any that keep to these rules, and one draw needn't show every extreme that they name: The panel has full column rank, its columns of differing scales.
All inputs are finite; a program needn't handle non-finite values.
Results may differ from the reference program's by a relative error of at most 0.0025.
Values sent between devices are 32-bit elements; how exact they have to be, the bound alone decides.
No kernel may reach another device: no remote copies, remote signals or barrier semaphores. Data moves between devices by JAX's collectives and lax.ppermute only.
A program may use at most 64 MiB of HBM per device.

```python
import jax
import jax.numpy as jnp
from jax import lax

B = 256
NB = 2048
M = 32768
N = 16384


def draw_panel(key, part):
    key_base = jax.random.fold_in(key, 11)
    key_rough = jax.random.fold_in(key, 12)
    key_scale = jax.random.fold_in(key, 13)
    positions = jnp.arange(M, dtype=jnp.float32)
    ramp = jnp.exp(jnp.log(3.0) * positions / M)
    rough = jnp.exp(jax.random.uniform(key_rough, (M,), jnp.float32, -0.25, 0.25))
    col_scale = jnp.exp(jax.random.uniform(key_scale, (B,), jnp.float32, 0.0, jnp.log(8.0)))
    base = jax.random.normal(key_base, (M, B), jnp.float32)
    return (base * (ramp * rough)[:, None] * col_scale[None, :]).astype(jnp.float32)


def block_scale(rng, shape, shards, least, high):
    gain, own = 1.0, jax.random.fold_in(rng, 6)
    for position, parts in shards:
        draws = jnp.exp(jax.random.uniform(jax.random.fold_in(own, position), (parts,), jnp.float32, least / len(shards), high / len(shards)))
        gain = gain * jnp.repeat(draws, shape[position] // parts).reshape([-1 if axis == position else 1 for axis in range(len(shape))])
    return gain


def noise(own_key, extent, spread, most, pieces=(), kind=jnp.bfloat16):
    entries = jax.random.normal(own_key, extent, jnp.float32) * spread
    if len(pieces) > 0:
        entries = block_scale(own_key, extent, pieces, -0.22, 0.18) * entries
    return jnp.clip(entries, min=-most, max=most).astype(kind)


def setup_inputs(seed: int = 0) -> dict:
    streams_of = jax.random.split(jax.random.key(seed), 3)
    panel = draw_panel(jax.random.fold_in(streams_of[2], 71), 0)
    trailing = noise(streams_of[1], (M, N), 1.0, 6.0, ((0, 32), (1, 8)))
    return dict(panel=panel, trailing=trailing)


def reference(panel, trailing):
    highest = lax.Precision.HIGHEST
    gram = jnp.dot(panel.T.astype(jnp.float32), panel.astype(jnp.float32), precision=highest, preferred_element_type=jnp.float32)
    lower = jnp.linalg.cholesky(gram)
    r_factor = lower.T
    basis = jax.scipy.linalg.solve_triangular(lower, panel.T, lower=True).T
    basis_low = basis.astype(jnp.bfloat16)

    def one_block(index):
        block = lax.dynamic_slice_in_dim(trailing, index * NB, NB, 1)
        top_block = jnp.dot(basis.T.astype(jnp.float32), block.astype(jnp.float32), precision=highest, preferred_element_type=jnp.float32)
        update = jnp.dot(basis_low.astype(jnp.float32), top_block.astype(jnp.bfloat16).astype(jnp.float32), preferred_element_type=jnp.float32)
        fresh = (block.astype(jnp.float32) - update).astype(jnp.bfloat16)
        return (top_block, fresh)
    top_blocks, fresh_blocks = lax.map(one_block, jnp.arange(N // NB, dtype=jnp.int32))
    top_rows = jnp.transpose(top_blocks, (1, 0, 2)).reshape(B, N)
    updated = jnp.transpose(fresh_blocks, (1, 0, 2)).reshape(M, N)
    return (r_factor, top_rows, updated)
```

```python
import jax
import jax.numpy as jnp
from jax import lax
from jax.experimental import pallas as pl
from jax.experimental.pallas import tpu as pltpu
from jax.sharding import PartitionSpec as P

F32 = jnp.float32
BF16 = jnp.bfloat16
HIGHEST = lax.Precision.HIGHEST
NX, NZ = 4, 8
B, ROWS, COLS, HALF = 256, 1024, 2048, 128

X_GROUPS = [[x * NZ + z for x in range(NX)] for z in range(NZ)]
Z_GROUPS = [[x * NZ + z for z in range(NZ)] for x in range(NX)]
Y_GROUPS = [[2 * y + core for y in range(4)] for core in range(2)]
SIBLING = [(c, c ^ 1) for c in range(8)]


def dot(a, b, contract, precision=None):
    return lax.dot_general(a, b, (contract, ((), ())), precision=precision, preferred_element_type=F32)


def product_kernel(core_ref, mine_ref, other_ref, trailing_ref, panel_t_ref, out_ref, parts):
    first = core_ref[0] == 0
    for y in range(4):
        mine, other = mine_ref[y], other_ref[y]
        panel_t_ref[64 * y:64 * y + 32] = jnp.where(first, mine, other)
        panel_t_ref[64 * y + 32:64 * y + 64] = jnp.where(first, other, mine)
    value = panel_t_ref[...]
    high = value.astype(BF16)
    rest = value - high.astype(F32)
    middle = rest.astype(BF16)
    parts[0:B] = high
    parts[B:2 * B] = middle
    parts[2 * B:] = (rest - middle.astype(F32)).astype(BF16)
    half = panel_t_ref[pl.ds(pl.multiple_of(core_ref[0] * HALF, HALF), HALF)]
    out_ref[:, COLS:] = dot(value, half, ((1,), (1,)), HIGHEST)

    @pl.loop(0, COLS // 256)
    def _(tile):
        columns = pl.ds(pl.multiple_of(tile * 256, 256), 256)
        block = trailing_ref[:, columns]
        total = dot(parts[2 * B:], block, ((1,), (0,)))
        total += dot(parts[B:2 * B], block, ((1,), (0,)))
        out_ref[:, columns] = total + dot(parts[0:B], block, ((1,), (0,)))


def eliminate(work, upper, inverse):
    n = HALF
    row = lax.broadcasted_iota(jnp.int32, (n, 1), 0)
    eight = lax.broadcasted_iota(jnp.int32, (8, 1), 0)
    lane = lax.broadcasted_iota(jnp.int32, (n, n), 1)
    inverse[...] = (lane == lax.broadcasted_iota(jnp.int32, (n, n), 0)).astype(F32)

    @pl.loop(0, n // 8)
    def _(block):
        base = pl.multiple_of(block * 8, 8)
        s = work[...]
        m = inverse[...]
        pivots = jnp.zeros((8, 1), F32)
        for k in range(8):
            pivot_s = jnp.sum(jnp.where(row == base + k, s, 0.0), axis=0, keepdims=True)
            pivot_m = jnp.sum(jnp.where(row == base + k, m, 0.0), axis=0, keepdims=True)
            pivot = pivot_s[:, k:k + 1]
            factor = jnp.where(row > base + k, s[:, k:k + 1] / pivot, 0.0)
            s = s - factor * pivot_s
            m = m - factor * pivot_m
            pivots = jnp.where(eight == k, pivot, pivots)
        work[...] = s
        inverse[...] = m
        scale = lax.rsqrt(pivots)
        scale = scale * (1.5 - 0.5 * pivots * scale * scale)
        inverse[pl.ds(base, 8)] = inverse[pl.ds(base, 8)] * scale
        upper[pl.ds(base, 8)] = pltpu.roll(work[pl.ds(base, 8)] * scale, base, 1)
        work[...] = pltpu.roll(work[...], n - 8, 1)

    inv = inverse[...]
    up = upper[...]
    sub = lax.broadcasted_iota(jnp.int32, (n, n), 0)
    upper[...] = jnp.where(lane >= sub, up, 0.0)
    inverse[...] = jnp.where(lane <= sub, inv, 0.0)


def factor_kernel(core_ref, mine_ref, other_ref, panel_t_ref, r_ref, inv_ref, low_ref, work, upper, inverse):
    first = core_ref[0] == 0
    mine, other = mine_ref[...], other_ref[...]
    left = jnp.where(first, mine, other)
    right = jnp.where(first, other, mine)
    work[...] = left[:HALF]
    eliminate(work, upper, inverse)
    r_ref[:HALF, :HALF] = upper[...]
    inv_ref[:HALF, :HALF] = inverse[...]
    inv_ref[:HALF, HALF:] = jnp.zeros((HALF, HALF), F32)
    r_ref[HALF:, :HALF] = jnp.zeros((HALF, HALF), F32)
    cross = dot(inverse[...], right[:HALF], ((1,), (0,)), HIGHEST)
    r_ref[:HALF, HALF:] = cross
    work[...] = right[HALF:] - dot(cross, cross, ((0,), (0,)), HIGHEST)
    eliminate(work, upper, inverse)
    r_ref[HALF:, HALF:] = upper[...]
    inv_ref[HALF:, HALF:] = inverse[...]
    lower = dot(cross, inv_ref[:HALF, :HALF], ((0,), (0,)), HIGHEST)
    inv_ref[HALF:, :HALF] = -dot(inverse[...], lower, ((1,), (0,)), HIGHEST)
    basis = dot(panel_t_ref[...], inv_ref[...], ((0,), (1,)), HIGHEST)
    low_ref[...] = basis.astype(BF16)


def update_kernel(sums_ref, inv_ref, low_ref, trailing_ref, top_ref, updated_ref):
    top = dot(inv_ref[...], sums_ref[...], ((1,), (0,)), HIGHEST)
    top_ref[...] = top
    change = dot(low_ref[...], top.astype(BF16), ((1,), (0,)))
    updated_ref[...] = (trailing_ref[...].astype(F32) - change).astype(BF16)


VMEM = pl.BlockSpec(memory_space=pltpu.VMEM)
SMEM = pl.BlockSpec(memory_space=pltpu.SMEM)


def cost(flops, size):
    return pl.CostEstimate(flops=int(flops), bytes_accessed=int(size), transcendentals=0)


def swap(block, axis, groups):
    return lax.all_to_all(block, axis, 0, 0, tiled=True, axis_index_groups=groups)


def gather(block, axis, groups):
    count = len(groups[0])
    return swap(jnp.concatenate([block] * count, axis=0), axis, groups)


def scatter_sum(block, axis, groups):
    count = len(groups[0])
    received = swap(block, axis, groups)
    return jnp.sum(received.reshape((count, -1) + block.shape[1:]), axis=0)


def local(panel, trailing):
    core = (lax.axis_index("col") % 2).astype(jnp.int32).reshape(1)
    params = pltpu.CompilerParams(vmem_limit_bytes=48 * 2**20)
    with jax.named_scope("gather_panel"):
        mine = gather(panel.T, "col", Y_GROUPS)
        other = lax.ppermute(mine, "col", SIBLING)
    with jax.named_scope("product"):
        panel_t, sums = pl.pallas_call(
            product_kernel,
            out_shape=(jax.ShapeDtypeStruct((B, ROWS), F32), jax.ShapeDtypeStruct((B, COLS + HALF), F32)),
            in_specs=[SMEM, VMEM, VMEM, VMEM],
            out_specs=(VMEM, VMEM),
            scratch_shapes=[pltpu.VMEM((3 * B, ROWS), BF16)],
            compiler_params=params,
            cost_estimate=cost(3.6e9, 8e6),
        )(core, mine.reshape(4, 32, ROWS), other.reshape(4, 32, ROWS), trailing)
    with jax.named_scope("sum_over_x"):
        sums = scatter_sum(sums, "row", X_GROUPS)
    with jax.named_scope("sum_over_z"):
        sums = scatter_sum(sums, "row", Z_GROUPS)
    with jax.named_scope("gather_gram"):
        gram_mine = gather(gather(sums[:, COLS:], "row", Z_GROUPS), "row", X_GROUPS)
        gram_other = lax.ppermute(gram_mine, "col", SIBLING)
    with jax.named_scope("gather_sums"):
        sums = gather(gather(sums[:, :COLS], "row", Z_GROUPS), "row", X_GROUPS)
    with jax.named_scope("factor"):
        r_factor, inverse, low = pl.pallas_call(
            factor_kernel,
            out_shape=(
                jax.ShapeDtypeStruct((B, B), F32),
                jax.ShapeDtypeStruct((B, B), F32),
                jax.ShapeDtypeStruct((ROWS, B), BF16),
            ),
            in_specs=[SMEM, VMEM, VMEM, VMEM],
            out_specs=(VMEM, VMEM, VMEM),
            scratch_shapes=[pltpu.VMEM((HALF, HALF), F32)] * 3,
            compiler_params=params,
            cost_estimate=cost(2e10, 3e6),
        )(core, gram_mine, gram_other, panel_t)
    with jax.named_scope("update"):
        tile = 256
        top, updated = pl.pallas_call(
            update_kernel,
            grid=(COLS // tile,),
            out_shape=(jax.ShapeDtypeStruct((B, COLS), F32), jax.ShapeDtypeStruct((ROWS, COLS), BF16)),
            in_specs=[
                pl.BlockSpec((B, tile), lambda i: (0, i)),
                pl.BlockSpec((B, B), lambda i: (0, 0)),
                pl.BlockSpec((ROWS, B), lambda i: (0, 0)),
                pl.BlockSpec((ROWS, tile), lambda i: (0, i)),
            ],
            out_specs=(
                pl.BlockSpec((B, tile), lambda i: (0, i)),
                pl.BlockSpec((ROWS, tile), lambda i: (0, i)),
            ),
            compiler_params=params,
            cost_estimate=cost(3e9, 12e6),
        )(sums, inverse, low, trailing)
    return r_factor, top, updated


def solution(mesh):
    return jax.shard_map(
        local,
        mesh=mesh,
        in_specs=(P("row", "col"), P("row", "col")),
        out_specs=(P(), P(None, "col"), P("row", "col")),
        check_vma=False,
    )
```

```python
import jax
import jax.numpy as jnp
from jax import lax
from jax.experimental import pallas as pl
from jax.experimental.pallas import tpu as pltpu
from jax.sharding import PartitionSpec as P

F32 = jnp.float32
BF16 = jnp.bfloat16
HIGHEST = lax.Precision.HIGHEST
NX, NZ = 4, 8
B, ROWS, COLS, HALF, TILE = 256, 1024, 2048, 128, 256
A_COLS, B_COLS = 1280, 768

Z_GROUPS = [[x * NZ + z for z in range(NZ)] for x in range(NX)]
Y_GROUPS = [[2 * y + core for y in range(4)] for core in range(2)]
SIBLING = [(c, c ^ 1) for c in range(8)]
X_ROUTES = [[(x * NZ + z, (x + k) % NX * NZ + z) for x in range(NX) for z in range(NZ)] for k in range(NX)]


def dot(a, b, contract=((1,), (0,)), precision=None):
    return lax.dot_general(a, b, (contract, ((), ())), precision=precision, preferred_element_type=F32)


def split(value, count):
    terms = []
    for _ in range(count):
        terms.append(value.astype(BF16))
        value = value - terms[-1].astype(F32)
    return terms


def dot_split(left, high, low):
    rows = left.shape[0] // 2
    both = dot(left, high)
    return both[rows:] + dot(left[:rows], low) + both[:rows]


def tile_of(index):
    return slice(index * TILE, index * TILE + TILE)


def fetches(source_ref, target_ref, first, count, arrived):
    copies = [
        pltpu.make_async_copy(source_ref.at[:, tile_of(first + tile)], target_ref.at[:, tile_of(tile)], arrived.at[tile])
        for tile in range(count)
    ]
    for copy in copies:
        copy.start()
    return copies


def product_a_kernel(ids_ref, mine_ref, other_ref, trailing_ref, parts_ref, *refs):
    pieces, (held, third, whole, gram, arrived) = refs[:NX], refs[NX:]
    copies = fetches(trailing_ref, held, 0, A_COLS // TILE, arrived)
    first = ids_ref[0] == 0
    for y in range(4):
        mine, other = mine_ref[y], other_ref[y]
        for offset, value in ((0, jnp.where(first, mine, other)), (32, jnp.where(first, other, mine))):
            start = 64 * y + offset
            high, middle, low = split(value, 3)
            parts_ref[start:start + 32] = high
            parts_ref[B + start:B + start + 32] = middle
            third[start:start + 32] = low
    half = pl.multiple_of(ids_ref[0] * HALF, HALF)
    last = ((1,), (1,))
    one = dot(parts_ref[...], parts_ref[pl.ds(half, HALF)], last)
    two = dot(parts_ref[...], parts_ref[pl.ds(pl.multiple_of(B + half, HALF), HALF)], last)
    small = dot(third[...], parts_ref[pl.ds(half, HALF)], last) + dot(parts_ref[:B], third[pl.ds(half, HALF)], last)
    gram[...] = small + two[B:] + one[B:] + two[:B] + one[:B]

    def hand_out(source, columns):
        for k in range(NX):
            start = pl.multiple_of(64 * lax.rem(ids_ref[1] + k, NX), 64)
            pieces[k][:, columns] = source[pl.ds(start, 64)]

    hand_out(gram, slice(A_COLS, A_COLS + HALF))
    for tile, copy in enumerate(copies):
        copy.wait()
        both = dot(parts_ref[...], held[:, tile_of(tile)])
        slot = whole.at[tile % 2]
        slot[...] = both[B:] + both[:B]
        hand_out(slot, tile_of(tile))


def product_b_kernel(parts_ref, trailing_ref, out_ref, held, arrived):
    copies = fetches(trailing_ref, held, A_COLS // TILE, B_COLS // TILE, arrived)
    for tile, copy in enumerate(copies):
        copy.wait()
        both = dot(parts_ref[...], held[:, tile_of(tile)])
        out_ref[:, tile_of(tile)] = both[B:] + both[:B]


def eliminate(work, unit, upper, inverse):
    n, tiles = HALF, HALF // 8
    shape = (tiles, 8, n)
    row = 8 * lax.broadcasted_iota(jnp.int32, shape, 0) + lax.broadcasted_iota(jnp.int32, shape, 1)
    lane = lax.broadcasted_iota(jnp.int32, shape, 2)
    eight = lax.broadcasted_iota(jnp.int32, (8, n), 0)
    unit[...] = (lane == row).astype(F32)

    def splat(tile, i, k):
        return jnp.broadcast_to(tile[i:i + 1, k:k + 1], (8, n))

    def reciprocal_root(value):
        guess = lax.rsqrt(value)
        return guess * (1.5 - 0.5 * value * guess * guess)

    @pl.loop(0, tiles)
    def _(block):
        s, m = work[...], unit[...]
        pivot_s, pivot_m = work[block], unit[block]
        done_s, done_m = pivot_s, pivot_m
        for half in (0, 4):
            p = {(i, k): splat(pivot_s, half + i, half + k) for i in range(4) for k in range(i + 1)}
            low, root, inv = {}, [], {}
            for k in range(4):
                for i in range(k, 4):
                    value = p[i, k]
                    for q in range(k):
                        value = value - low[i, q] * low[k, q]
                    if i == k:
                        root.append(reciprocal_root(value))
                    else:
                        low[i, k] = value * root[k]
            for i in range(4):
                inv[i, i] = root[i]
                for k in range(i):
                    value = low[i, k] * inv[k, k]
                    for q in range(k + 1, i):
                        value = value + low[i, q] * inv[q, k]
                    inv[i, k] = -value * root[i]

            def combine(items):
                out = []
                for i in range(4):
                    value = inv[i, 0] * items[0]
                    for k in range(1, i + 1):
                        value = value + inv[i, k] * items[k]
                    out.append(value)
                return out

            rows_s = combine([jnp.broadcast_to(pivot_s[half + k:half + k + 1], (8, n)) for k in range(4)])
            rows_m = combine([jnp.broadcast_to(pivot_m[half + k:half + k + 1], (8, n)) for k in range(4)])
            for k in range(4):
                done_s = jnp.where(eight == half + k, rows_s[k], done_s)
                done_m = jnp.where(eight == half + k, rows_m[k], done_m)
            if half == 0:
                factors = combine([jnp.broadcast_to(pivot_s[:, k:k + 1], (8, n)) for k in range(4)])
                for k in range(4):
                    pivot_s = pivot_s - factors[k] * rows_s[k]
                    pivot_m = pivot_m - factors[k] * rows_m[k]
            below = row > 8 * block + half + 3
            factors = combine([jnp.broadcast_to(s[:, :, half + k:half + k + 1], shape) for k in range(4)])
            for k in range(4):
                factor = jnp.where(below, factors[k], 0.0)
                s = s - factor * rows_s[k]
                m = m - factor * rows_m[k]
        upper[block] = pltpu.roll(done_s, 8 * block, 1)
        inverse[block] = done_m
        work[...] = pltpu.roll(s, n - 8, 2)
        unit[...] = m

    upper[...] = jnp.where(lane >= row, upper[...], 0.0)
    inverse[...] = jnp.where(lane <= row, inverse[...], 0.0)


def factor_kernel(ids_ref, mine_ref, other_ref, parts_ref, r_ref, inv_out_ref, low_out_ref,
                  work, unit, upper, inverse, inv_ref, low_ref, sent):
    tiled, flat = (HALF // 8, 8, HALF), (HALF, HALF)
    first = ids_ref[0] == 0
    for k in range(NX):
        rows = pl.ds(pl.multiple_of(64 * lax.rem(ids_ref[1] + NX - k, NX), 64), 64)
        mine, other = mine_ref[k], other_ref[k]
        r_ref[rows, :HALF] = jnp.where(first, mine, other)
        r_ref[rows, HALF:] = jnp.where(first, other, mine)
    right = r_ref[:, HALF:]
    work[...] = r_ref[:HALF, :HALF].reshape(tiled)
    eliminate(work, unit, upper, inverse)
    r_ref[:HALF, :HALF] = upper[...].reshape(flat)
    inverse_1 = inverse[...].reshape(flat)
    r_ref[HALF:, :HALF] = jnp.zeros(flat, F32)
    cross = dot(inverse_1, right[:HALF], precision=HIGHEST)
    r_ref[:HALF, HALF:] = cross
    work[...] = (right[HALF:] - dot(cross, cross, ((0,), (0,)), HIGHEST)).reshape(tiled)
    lower = dot(cross, inverse_1, ((0,), (0,)), HIGHEST)
    eliminate(work, unit, upper, inverse)
    r_ref[HALF:, HALF:] = upper[...].reshape(flat)
    inverse_2 = inverse[...].reshape(flat)
    below = -dot(inverse_2, lower, precision=HIGHEST)
    zero = jnp.zeros(flat, BF16)
    for start, one, two, three in zip((0, B), split(inverse_1, 2), split(below, 2), split(inverse_2, 2)):
        inv_ref[start:start + HALF, :HALF] = one
        inv_ref[start:start + HALF, HALF:] = zero
        inv_ref[start + HALF:start + B, :HALF] = two
        inv_ref[start + HALF:start + B, HALF:] = three
    basis = dot_split(inv_ref[...], parts_ref[:B], parts_ref[B:])
    low_ref[...] = basis.T.astype(BF16)
    results = [
        pltpu.make_async_copy(inv_ref, inv_out_ref, sent.at[0]),
        pltpu.make_async_copy(low_ref, low_out_ref, sent.at[1]),
    ]
    for result in results:
        result.start()
    for result in results:
        result.wait()


def update_kernel(ids_ref, a0_ref, a1_ref, a2_ref, a3_ref, b_ref, inv_in_ref, low_in_ref, trailing_ref,
                  top_ref, updated_ref, inv_ref, low_ref, sums, held, top, updated, ready, arrived, sent):
    inputs = [
        pltpu.make_async_copy(inv_in_ref, inv_ref, ready.at[0]),
        pltpu.make_async_copy(low_in_ref, low_ref, ready.at[1]),
    ]
    for copy in inputs:
        copy.start()
    copies = fetches(trailing_ref, held, 0, COLS // TILE, arrived)
    for k, a_ref in enumerate((a0_ref, a1_ref, a2_ref, a3_ref)):
        x = lax.rem(ids_ref[1] + NX - k, NX)
        sums[pl.ds(pl.multiple_of(64 * x, 64), 64), :A_COLS] = a_ref[...]
        for z in range(NZ):
            sums[pl.ds(pl.multiple_of(32 * z + 8 * x, 8), 8), A_COLS:] = b_ref[z, k]
    for copy in inputs:
        copy.wait()
    results = []

    def send(source, target, semaphore):
        results.append(pltpu.make_async_copy(source, target, semaphore))
        results[-1].start()

    for tile in range(COLS // TILE):
        columns = tile_of(tile)
        rows = dot_split(inv_ref[...], *split(sums[:, columns], 2))
        top[:, columns] = rows
        send(top.at[:, columns], top_ref.at[:, columns], sent.at[0, tile])
        change = dot(low_ref[...], rows.astype(BF16))
        copies[tile].wait()
        updated[:, columns] = (held[:, columns].astype(F32) - change).astype(BF16)
        send(updated.at[:, columns], updated_ref.at[:, columns], sent.at[1, tile])
    for result in results:
        result.wait()


HBM = pl.BlockSpec(memory_space=pltpu.HBM)
VMEM = pl.BlockSpec(memory_space=pltpu.VMEM)
SMEM = pl.BlockSpec(memory_space=pltpu.SMEM)


def cost(flops, size):
    return pl.CostEstimate(flops=int(flops), bytes_accessed=int(size), transcendentals=0)


def limit(mib):
    return pltpu.CompilerParams(vmem_limit_bytes=mib * 2**20)


def array(*shape, dtype=F32):
    return jax.ShapeDtypeStruct(shape, dtype)


def product_a(ids, mine, other, trailing):
    tiles = A_COLS // TILE
    return pl.pallas_call(
        product_a_kernel,
        out_shape=(array(2 * B, ROWS, dtype=BF16),) + (array(B // NX, A_COLS + HALF),) * NX,
        in_specs=[SMEM, VMEM, VMEM, HBM],
        out_specs=(VMEM,) * (1 + NX),
        scratch_shapes=[
            pltpu.VMEM((ROWS, A_COLS), BF16),
            pltpu.VMEM((B, ROWS), BF16),
            pltpu.VMEM((2, B, TILE), F32),
            pltpu.VMEM((B, HALF), F32),
            pltpu.SemaphoreType.DMA((tiles,)),
        ],
        compiler_params=limit(50),
        cost_estimate=cost(2.4e9, 6e6),
    )(ids, mine.reshape(4, 32, ROWS), other.reshape(4, 32, ROWS), trailing)


def product_b(parts, trailing):
    tiles = B_COLS // TILE
    return pl.pallas_call(
        product_b_kernel,
        out_shape=array(B, B_COLS),
        in_specs=[VMEM, HBM],
        out_specs=VMEM,
        scratch_shapes=[pltpu.VMEM((ROWS, B_COLS), BF16), pltpu.SemaphoreType.DMA((tiles,))],
        compiler_params=limit(50),
        cost_estimate=cost(1.3e9, 4e6),
    )(parts, trailing)


def factor(ids, mine, other, parts):
    return pl.pallas_call(
        factor_kernel,
        out_shape=(
            array(B, B),
            array(2 * B, B, dtype=BF16),
            array(ROWS, B, dtype=BF16),
        ),
        in_specs=[SMEM, VMEM, VMEM, VMEM],
        out_specs=(VMEM, HBM, HBM),
        scratch_shapes=[pltpu.VMEM((HALF // 8, 8, HALF), F32)] * 4
        + [pltpu.VMEM((2 * B, B), BF16), pltpu.VMEM((ROWS, B), BF16), pltpu.SemaphoreType.DMA((2,))],
        compiler_params=limit(20),
        cost_estimate=cost(2e10, 3e6),
    )(ids, mine, other, parts)


def update(ids, a, b, inverse, low, trailing):
    tiles = COLS // TILE
    return pl.pallas_call(
        update_kernel,
        out_shape=(array(B, COLS), array(ROWS, COLS, dtype=BF16)),
        in_specs=[SMEM] + [VMEM] * 5 + [HBM] * 3,
        out_specs=(HBM, HBM),
        scratch_shapes=[
            pltpu.VMEM((2 * B, B), BF16),
            pltpu.VMEM((ROWS, B), BF16),
            pltpu.VMEM((B, COLS), F32),
            pltpu.VMEM((ROWS, COLS), BF16),
            pltpu.VMEM((B, COLS), F32),
            pltpu.VMEM((ROWS, COLS), BF16),
            pltpu.SemaphoreType.DMA((2,)),
            pltpu.SemaphoreType.DMA((tiles,)),
            pltpu.SemaphoreType.DMA((2, tiles)),
        ],
        compiler_params=limit(50),
        cost_estimate=cost(3e9, 12e6),
    )(ids, *a, b, inverse, low, trailing)


def swap(block, axis, groups):
    return lax.all_to_all(block, axis, 0, 0, axis_index_groups=groups)


def gather(block, axis, groups):
    return swap(jnp.broadcast_to(block[None], (len(groups[0]),) + block.shape), axis, groups)


def scatter_z(block):
    return swap(block.reshape((NZ, -1) + block.shape[1:]), "row", Z_GROUPS)


def shift_x(pieces):
    return [pieces[0]] + [lax.ppermute(pieces[k], "row", X_ROUTES[k]) for k in range(1, NX)]


def local(panel, trailing):
    x = lax.axis_index("row") // NZ
    ids = jnp.stack([lax.axis_index("col") % 2, x]).astype(jnp.int32)
    with jax.named_scope("gather_panel"):
        mine = gather(panel.T, "col", Y_GROUPS)
        other = lax.ppermute(mine, "col", SIBLING)
    with jax.named_scope("product"):
        parts, *a = product_a(ids, mine, other, trailing)
        b = product_b(parts, trailing)
    together = lax.optimization_barrier
    with jax.named_scope("sum_first"):
        a, b = together((shift_x(a), scatter_z(b)))
        a, b = together((sum(a), jnp.sum(b, axis=0)))
    with jax.named_scope("sum_second"):
        b = shift_x([lax.dynamic_slice_in_dim(b, (x + k) % NX * 8, 8, 0) for k in range(NX)])
        a, b = together((scatter_z(a), b))
        a, b = together((jnp.sum(a, axis=0), sum(b)))
    with jax.named_scope("gather_first"):
        a, b = together((gather(a, "row", Z_GROUPS), shift_x([b] * NX)))
        a, b = a.reshape(64, A_COLS + HALF), jnp.concatenate(b, axis=0)
    with jax.named_scope("gather_gram"):
        gram_mine = jnp.stack(shift_x([a[:, A_COLS:]] * NX))
        gram_other = lax.ppermute(gram_mine, "col", SIBLING)
    with jax.named_scope("gather_second"):
        a = shift_x([a[:, :A_COLS]] * NX)
        b = gather(b, "row", Z_GROUPS).reshape(NZ, NX, 8, B_COLS)
    with jax.named_scope("factor"):
        r_factor, inverse, low = factor(ids, gram_mine, gram_other, parts)
    with jax.named_scope("update"):
        top, updated = update(ids, a, b, inverse, low, trailing)
    return r_factor, top, updated


def solution(mesh):
    return jax.shard_map(
        local,
        mesh=mesh,
        in_specs=(P("row", "col"), P("row", "col")),
        out_specs=(P(), P(None, "col"), P("row", "col")),
        check_vma=False,
    )
```

```python
import functools

import jax
import jax.numpy as jnp
from jax import lax
from jax.experimental import pallas as pl
from jax.experimental.pallas import tpu as pltpu
from jax.sharding import PartitionSpec as P

F32 = jnp.float32
BF16 = jnp.bfloat16
HIGHEST = lax.Precision.HIGHEST
NX, NZ = 4, 8
B, ROWS, COLS, HALF, TILE = 256, 1024, 2048, 128, 256
A_COLS, B_COLS = 1280, 768
WIDE = 4

Z_GROUPS = [[x * NZ + z for z in range(NZ)] for x in range(NX)]
Y_GROUPS = [[2 * y + core for y in range(4)] for core in range(2)]
SIBLING = [(c, c ^ 1) for c in range(8)]
X_ROUTES = [[(x * NZ + z, (x + k) % NX * NZ + z) for x in range(NX) for z in range(NZ)] for k in range(NX)]


def dot(a, b, contract=((1,), (0,)), precision=None):
    return lax.dot_general(a, b, (contract, ((), ())), precision=precision, preferred_element_type=F32)


def split(value, count):
    terms = []
    for _ in range(count):
        terms.append(value.astype(BF16))
        value = value - terms[-1].astype(F32)
    return terms


def dot_split(left, high, low):
    rows = left.shape[0] // 2
    both = dot(left, high)
    return both[rows:] + dot(left[:rows], low) + both[:rows]


def tile_of(index):
    return slice(index * TILE, index * TILE + TILE)


def fetches(source_ref, target_ref, first, count, arrived):
    copies = [
        pltpu.make_async_copy(source_ref.at[:, tile_of(first + tile)], target_ref.at[:, tile_of(tile)], arrived.at[tile])
        for tile in range(count)
    ]
    for copy in copies:
        copy.start()
    return copies


def product_a_kernel(ids_ref, mine_ref, other_ref, trailing_ref, parts_ref, *refs):
    pieces, (held, third, whole, gram, arrived) = refs[:NX], refs[NX:]
    copies = fetches(trailing_ref, held, 0, A_COLS // TILE, arrived)
    first = ids_ref[0] == 0
    for y in range(4):
        mine, other = mine_ref[y], other_ref[y]
        for offset, value in ((0, jnp.where(first, mine, other)), (32, jnp.where(first, other, mine))):
            start = 64 * y + offset
            high, middle, low = split(value, 3)
            parts_ref[start:start + 32] = high
            parts_ref[B + start:B + start + 32] = middle
            third[start:start + 32] = low
    half = pl.multiple_of(ids_ref[0] * HALF, HALF)
    last = ((1,), (1,))
    one = dot(parts_ref[...], parts_ref[pl.ds(half, HALF)], last)
    two = dot(parts_ref[...], parts_ref[pl.ds(pl.multiple_of(B + half, HALF), HALF)], last)
    small = dot(third[...], parts_ref[pl.ds(half, HALF)], last) + dot(parts_ref[:B], third[pl.ds(half, HALF)], last)
    gram[...] = small + two[B:] + one[B:] + two[:B] + one[:B]

    def hand_out(source, columns):
        for k in range(NX):
            start = pl.multiple_of(64 * lax.rem(ids_ref[1] + k, NX), 64)
            pieces[k][:, columns] = source[pl.ds(start, 64)]

    hand_out(gram, slice(A_COLS, A_COLS + HALF))
    for tile, copy in enumerate(copies):
        copy.wait()
        both = dot(parts_ref[...], held[:, tile_of(tile)])
        slot = whole.at[tile % 2]
        slot[...] = both[B:] + both[:B]
        hand_out(slot, tile_of(tile))


def product_b_kernel(parts_ref, trailing_ref, out_ref, held, arrived):
    copies = fetches(trailing_ref, held, A_COLS // TILE, B_COLS // TILE, arrived)
    for copy in copies:
        copy.wait()
    both = dot(parts_ref[...], held[...])
    out_ref[...] = both[B:] + both[:B]


def eliminate(work, unit, upper, inverse):
    n, tiles = HALF, HALF // 8
    shape = (tiles, 8, n)
    row = 8 * lax.broadcasted_iota(jnp.int32, shape, 0) + lax.broadcasted_iota(jnp.int32, shape, 1)
    lane = lax.broadcasted_iota(jnp.int32, shape, 2)
    eight = lax.broadcasted_iota(jnp.int32, (8, n), 0)
    unit[...] = (lane == row).astype(F32)

    def reciprocal_root(value):
        guess = lax.rsqrt(value)
        return guess * (1.5 - 0.5 * value * guess * guess)

    def total(terms):
        while len(terms) > 1:
            terms = [sum(terms[at:at + 2]) for at in range(0, len(terms), 2)]
        return terms[0]

    def step(block, rest):
        pivot_s, pivot_m = work[block], unit[block]
        rows_s = [jnp.broadcast_to(pivot_s[k:k + 1], (8, n)) for k in range(8)]
        rows_m = [jnp.broadcast_to(pivot_m[k:k + 1], (8, n)) for k in range(8)]
        value = {(i, k): jnp.broadcast_to(pivot_s[i:i + 1, k:k + 1], (8, n)) for i in range(8) for k in range(i + 1)}
        low, inv = {}, {}
        for k in range(8):
            root = reciprocal_root(value[k, k])
            for i in range(k + 1, 8):
                low[i, k] = value[i, k] * root
            for i in range(k + 1, 8):
                for q in range(k + 1, i + 1):
                    value[i, q] = value[i, q] - low[i, k] * low[q, k]
            inv[k, k] = root
            for q in range(k):
                inv[k, q] = -root * total([low[k, t] * inv[t, q] for t in range(q, k)])

        def scaled(items):
            return [total([inv[i, k] * items[k] for k in range(i + 1)]) for i in range(8)]

        def solved(items):
            return [total([inv[i, k] * items[i] for i in range(k, 8)]) for k in range(8)]

        rows_s, rows_m = scaled(rows_s), scaled(rows_m)
        done_s, done_m = rows_s[0], rows_m[0]
        for k in range(1, 8):
            done_s = jnp.where(eight == k, rows_s[k], done_s)
            done_m = jnp.where(eight == k, rows_m[k], done_m)
        upper[block] = pltpu.roll(done_s, 8 * block, 1)
        inverse[block] = done_m
        s, m = work[rest], unit[rest]
        columns = [jnp.broadcast_to(s[:, :, k:k + 1], s.shape) for k in range(8)]
        for column, change_s, change_m in zip(columns, solved(rows_s), solved(rows_m)):
            s = s - column * change_s
            m = m - column * change_m
        work[rest] = pltpu.roll(s, n - 8, 2)
        unit[rest] = m

    for part in range(0, tiles, 4):
        pl.loop(part, part + 4)(functools.partial(step, rest=slice(part, tiles)))

    upper[...] = jnp.where(lane >= row, upper[...], 0.0)
    inverse[...] = jnp.where(lane <= row, inverse[...], 0.0)


def factor_kernel(ids_ref, mine_ref, other_ref, parts_ref, r_ref, inv_out_ref, low_out_ref,
                  work, unit, upper, inverse, inv_ref, low_ref, sent):
    tiled, flat = (HALF // 8, 8, HALF), (HALF, HALF)
    first = ids_ref[0] == 0
    for k in range(NX):
        rows = pl.ds(pl.multiple_of(64 * lax.rem(ids_ref[1] + NX - k, NX), 64), 64)
        mine, other = mine_ref[k], other_ref[k]
        r_ref[rows, :HALF] = jnp.where(first, mine, other)
        r_ref[rows, HALF:] = jnp.where(first, other, mine)
    right = r_ref[:, HALF:]
    work[...] = r_ref[:HALF, :HALF].reshape(tiled)
    eliminate(work, unit, upper, inverse)
    r_ref[:HALF, :HALF] = upper[...].reshape(flat)
    inverse_1 = inverse[...].reshape(flat)
    r_ref[HALF:, :HALF] = jnp.zeros(flat, F32)
    cross = dot(inverse_1, right[:HALF], precision=HIGHEST)
    r_ref[:HALF, HALF:] = cross
    work[...] = (right[HALF:] - dot(cross, cross, ((0,), (0,)), HIGHEST)).reshape(tiled)
    lower = dot(cross, inverse_1, ((0,), (0,)), HIGHEST)
    eliminate(work, unit, upper, inverse)
    r_ref[HALF:, HALF:] = upper[...].reshape(flat)
    inverse_2 = inverse[...].reshape(flat)
    below = -dot(inverse_2, lower, precision=HIGHEST)
    zero = jnp.zeros(flat, BF16)
    for start, one, two, three in zip((0, B), split(inverse_1, 2), split(below, 2), split(inverse_2, 2)):
        inv_ref[start:start + HALF, :HALF] = one
        inv_ref[start:start + HALF, HALF:] = zero
        inv_ref[start + HALF:start + B, :HALF] = two
        inv_ref[start + HALF:start + B, HALF:] = three
    basis = dot_split(inv_ref[...], parts_ref[:B], parts_ref[B:])
    low_ref[...] = basis.T.astype(BF16)
    results = [
        pltpu.make_async_copy(inv_ref, inv_out_ref, sent.at[0]),
        pltpu.make_async_copy(low_ref, low_out_ref, sent.at[1]),
    ]
    for result in results:
        result.start()
    for result in results:
        result.wait()


def update_kernel(ids_ref, a0_ref, a1_ref, a2_ref, a3_ref, b_ref, inv_in_ref, low_in_ref, trailing_ref,
                  top_ref, updated_ref, inv_ref, low_ref, sums, held, top, updated, ready, arrived, sent):
    inputs = [
        pltpu.make_async_copy(inv_in_ref, inv_ref, ready.at[0]),
        pltpu.make_async_copy(low_in_ref, low_ref, ready.at[1]),
    ]
    for copy in inputs:
        copy.start()
    copies = fetches(trailing_ref, held, 0, COLS // TILE, arrived)
    for k, a_ref in enumerate((a0_ref, a1_ref, a2_ref, a3_ref)):
        x = lax.rem(ids_ref[1] + NX - k, NX)
        sums[pl.ds(pl.multiple_of(64 * x, 64), 64), :A_COLS] = a_ref[...]
        for z in range(NZ):
            sums[pl.ds(pl.multiple_of(32 * z + 8 * x, 8), 8), A_COLS:] = b_ref[z, k]
    for copy in inputs:
        copy.wait()
    results = []

    def send(source, target, semaphore):
        results.append(pltpu.make_async_copy(source, target, semaphore))
        results[-1].start()

    for tile in range(0, COLS // TILE, WIDE):
        columns = slice(tile * TILE, (tile + WIDE) * TILE)
        rows = dot_split(inv_ref[...], *split(sums[:, columns], 2))
        top[:, columns] = rows
        send(top.at[:, columns], top_ref.at[:, columns], sent.at[0, tile])
        change = dot(low_ref[...], rows.astype(BF16))
        for copy in copies[tile:tile + WIDE]:
            copy.wait()
        updated[:, columns] = (held[:, columns].astype(F32) - change).astype(BF16)
        send(updated.at[:, columns], updated_ref.at[:, columns], sent.at[1, tile])
    for result in results:
        result.wait()


HBM = pl.BlockSpec(memory_space=pltpu.HBM)
VMEM = pl.BlockSpec(memory_space=pltpu.VMEM)
SMEM = pl.BlockSpec(memory_space=pltpu.SMEM)


def cost(flops, size):
    return pl.CostEstimate(flops=int(flops), bytes_accessed=int(size), transcendentals=0)


def limit(mib):
    return pltpu.CompilerParams(vmem_limit_bytes=mib * 2**20)


def array(*shape, dtype=F32):
    return jax.ShapeDtypeStruct(shape, dtype)


def product_a(ids, mine, other, trailing):
    tiles = A_COLS // TILE
    return pl.pallas_call(
        product_a_kernel,
        out_shape=(array(2 * B, ROWS, dtype=BF16),) + (array(B // NX, A_COLS + HALF),) * NX,
        in_specs=[SMEM, VMEM, VMEM, HBM],
        out_specs=(VMEM,) * (1 + NX),
        scratch_shapes=[
            pltpu.VMEM((ROWS, A_COLS), BF16),
            pltpu.VMEM((B, ROWS), BF16),
            pltpu.VMEM((2, B, TILE), F32),
            pltpu.VMEM((B, HALF), F32),
            pltpu.SemaphoreType.DMA((tiles,)),
        ],
        compiler_params=limit(50),
        cost_estimate=cost(2.4e9, 6e6),
    )(ids, mine.reshape(4, 32, ROWS), other.reshape(4, 32, ROWS), trailing)


def product_b(parts, trailing):
    tiles = B_COLS // TILE
    return pl.pallas_call(
        product_b_kernel,
        out_shape=array(B, B_COLS),
        in_specs=[VMEM, HBM],
        out_specs=VMEM,
        scratch_shapes=[pltpu.VMEM((ROWS, B_COLS), BF16), pltpu.SemaphoreType.DMA((tiles,))],
        compiler_params=limit(50),
        cost_estimate=cost(1.3e9, 4e6),
    )(parts, trailing)


def factor(ids, mine, other, parts):
    return pl.pallas_call(
        factor_kernel,
        out_shape=(
            array(B, B),
            array(2 * B, B, dtype=BF16),
            array(ROWS, B, dtype=BF16),
        ),
        in_specs=[SMEM, VMEM, VMEM, VMEM],
        out_specs=(VMEM, HBM, HBM),
        scratch_shapes=[pltpu.VMEM((HALF // 8, 8, HALF), F32)] * 4
        + [pltpu.VMEM((2 * B, B), BF16), pltpu.VMEM((ROWS, B), BF16), pltpu.SemaphoreType.DMA((2,))],
        compiler_params=limit(20),
        cost_estimate=cost(2e10, 3e6),
    )(ids, mine, other, parts)


def update(ids, a, b, inverse, low, trailing):
    tiles = COLS // TILE
    return pl.pallas_call(
        update_kernel,
        out_shape=(array(B, COLS), array(ROWS, COLS, dtype=BF16)),
        in_specs=[SMEM] + [VMEM] * 5 + [HBM] * 3,
        out_specs=(HBM, HBM),
        scratch_shapes=[
            pltpu.VMEM((2 * B, B), BF16),
            pltpu.VMEM((ROWS, B), BF16),
            pltpu.VMEM((B, COLS), F32),
            pltpu.VMEM((ROWS, COLS), BF16),
            pltpu.VMEM((B, COLS), F32),
            pltpu.VMEM((ROWS, COLS), BF16),
            pltpu.SemaphoreType.DMA((2,)),
            pltpu.SemaphoreType.DMA((tiles,)),
            pltpu.SemaphoreType.DMA((2, tiles)),
        ],
        compiler_params=limit(50),
        cost_estimate=cost(3e9, 12e6),
    )(ids, *a, b, inverse, low, trailing)


def swap(block, axis, groups):
    return lax.all_to_all(block, axis, 0, 0, axis_index_groups=groups)


def gather(block, axis, groups):
    return swap(jnp.broadcast_to(block[None], (len(groups[0]),) + block.shape), axis, groups)


def scatter_z(block):
    return swap(block.reshape((NZ, -1) + block.shape[1:]), "row", Z_GROUPS)


def shift_x(pieces):
    return [pieces[0]] + [lax.ppermute(pieces[k], "row", X_ROUTES[k]) for k in range(1, NX)]


def local(panel, trailing):
    x = lax.axis_index("row") // NZ
    ids = jnp.stack([lax.axis_index("col") % 2, x]).astype(jnp.int32)
    with jax.named_scope("gather_panel"):
        mine = gather(panel.T, "col", Y_GROUPS)
        other = lax.ppermute(mine, "col", SIBLING)
    with jax.named_scope("product"):
        parts, *a = product_a(ids, mine, other, trailing)
        b = product_b(parts, trailing)
    together = lax.optimization_barrier
    with jax.named_scope("sum_first"):
        a, b = together((shift_x(a), scatter_z(b)))
        a, b = together((sum(a), jnp.sum(b, axis=0)))
        a, gram = a[:, :A_COLS], a[:, A_COLS:]
    with jax.named_scope("sum_second"):
        b = shift_x([lax.dynamic_slice_in_dim(b, (x + k) % NX * 8, 8, 0) for k in range(NX)])
        a = scatter_z(a)
        for apart in (1, 2, 4):
            gram = gram + lax.ppermute(gram, "row", [(r, r ^ apart) for r in range(NX * NZ)])
        a, b, gram = together((a, b, gram))
        a, b = together((jnp.sum(a, axis=0), sum(b)))
    with jax.named_scope("gather_first"):
        gram_mine = jnp.stack(shift_x([gram] * NX))
        gram_other = lax.ppermute(gram_mine, "col", SIBLING)
        a, b, gram_mine, gram_other = together(
            (gather(a, "row", Z_GROUPS), shift_x([b] * NX), gram_mine, gram_other)
        )
    with jax.named_scope("gather_second"):
        a = shift_x([a.reshape(64, A_COLS)] * NX)
        b = gather(jnp.concatenate(b, axis=0), "row", Z_GROUPS).reshape(NZ, NX, 8, B_COLS)
    with jax.named_scope("factor"):
        r_factor, inverse, low = factor(ids, gram_mine, gram_other, parts)
    with jax.named_scope("update"):
        top, updated = update(ids, a, b, inverse, low, trailing)
    return r_factor, top, updated


def solution(mesh):
    return jax.shard_map(
        local,
        mesh=mesh,
        in_specs=(P("row", "col"), P("row", "col")),
        out_specs=(P(), P(None, "col"), P("row", "col")),
        check_vma=False,
    )
```

```python
import functools

import jax
import jax.numpy as jnp
from jax import lax
from jax.experimental import pallas as pl
from jax.experimental.pallas import tpu as pltpu
from jax.sharding import PartitionSpec as P

F32 = jnp.float32
BF16 = jnp.bfloat16
HIGHEST = lax.Precision.HIGHEST
NX, NZ = 4, 8
B, ROWS, COLS, HALF, TILE = 256, 1024, 2048, 128, 256
WIDE = 4

Z_GROUPS = [[x * NZ + z for z in range(NZ)] for x in range(NX)]
SIBLING = [(c, c ^ 1) for c in range(8)]
Y_ROUTES = [[(c, (c + 2 * k) % 8) for c in range(8)] for k in range(4)]
X_ROUTES = [[(x * NZ + z, (x + k) % NX * NZ + z) for x in range(NX) for z in range(NZ)] for k in range(NX)]


def dot(a, b, contract=((1,), (0,)), precision=None):
    return lax.dot_general(a, b, (contract, ((), ())), precision=precision, preferred_element_type=F32)


def split(value, count):
    terms = []
    for _ in range(count):
        terms.append(value.astype(BF16))
        value = value - terms[-1].astype(F32)
    return terms


def dot_split(left, high, low):
    rows = left.shape[0] // 2
    both = dot(left, high)
    return both[rows:] + dot(left[:rows], low) + both[:rows]


def tile_of(index):
    return slice(index * TILE, index * TILE + TILE)


def fetches(source_ref, target_ref, arrived):
    copies = [
        pltpu.make_async_copy(source_ref.at[:, tile_of(tile)], target_ref.at[:, tile_of(tile)], arrived.at[tile])
        for tile in range(COLS // TILE)
    ]
    for copy in copies:
        copy.start()
    return copies


def product_kernel(ids_ref, mine_ref, other_ref, trailing_ref, parts_ref, *refs):
    pieces, (held, third, whole, gram, arrived) = refs[:NX], refs[NX:]
    copies = fetches(trailing_ref, held, arrived)
    core, x, y = ids_ref[0], ids_ref[1], ids_ref[2]
    for k in range(4):
        for ref, offset in ((mine_ref, 32 * core), (other_ref, 32 - 32 * core)):
            start = 64 * lax.rem(y + 4 - k, 4) + offset
            high, middle, low = split(ref[k], 3)
            parts_ref[pl.ds(pl.multiple_of(start, 32), 32)] = high
            parts_ref[pl.ds(pl.multiple_of(B + start, 32), 32)] = middle
            third[pl.ds(pl.multiple_of(start, 32), 32)] = low
    half = pl.multiple_of(core * HALF, HALF)
    last = ((1,), (1,))
    one = dot(parts_ref[...], parts_ref[pl.ds(half, HALF)], last)
    two = dot(parts_ref[...], parts_ref[pl.ds(pl.multiple_of(B + half, HALF), HALF)], last)
    small = dot(third[...], parts_ref[pl.ds(half, HALF)], last) + dot(parts_ref[:B], third[pl.ds(half, HALF)], last)
    gram[...] = small + two[B:] + one[B:] + two[:B] + one[:B]

    def hand_out(source, columns):
        for k in range(NX):
            start = pl.multiple_of(64 * lax.rem(x + k, NX), 64)
            pieces[k][:, columns] = source[pl.ds(start, 64)]

    hand_out(gram, slice(COLS, COLS + HALF))
    for tile in range(0, COLS // TILE, 2):
        for copy in copies[tile:tile + 2]:
            copy.wait()
        columns = slice(tile * TILE, (tile + 2) * TILE)
        both = dot(parts_ref[...], held[:, columns])
        slot = whole.at[tile // 2 % 2]
        slot[...] = both[B:] + both[:B]
        hand_out(slot, columns)


def eliminate(work, unit, upper, inverse):
    n, tiles = HALF, HALF // 8
    shape = (tiles, 8, n)
    row = 8 * lax.broadcasted_iota(jnp.int32, shape, 0) + lax.broadcasted_iota(jnp.int32, shape, 1)
    lane = lax.broadcasted_iota(jnp.int32, shape, 2)
    eight = lax.broadcasted_iota(jnp.int32, (8, n), 0)
    unit[...] = (lane == row).astype(F32)

    def reciprocal_root(value):
        guess = lax.rsqrt(value)
        return guess * (1.5 - 0.5 * value * guess * guess)

    def total(terms):
        while len(terms) > 1:
            terms = [sum(terms[at:at + 2]) for at in range(0, len(terms), 2)]
        return terms[0]

    def step(block, rest):
        pivot_s, pivot_m = work[block], unit[block]
        rows_s = [jnp.broadcast_to(pivot_s[k:k + 1], (8, n)) for k in range(8)]
        rows_m = [jnp.broadcast_to(pivot_m[k:k + 1], (8, n)) for k in range(8)]
        value = {(i, k): jnp.broadcast_to(pivot_s[i:i + 1, k:k + 1], (8, n)) for i in range(8) for k in range(i + 1)}
        low, inv = {}, {}
        for k in range(8):
            root = reciprocal_root(value[k, k])
            for i in range(k + 1, 8):
                low[i, k] = value[i, k] * root
            for i in range(k + 1, 8):
                for q in range(k + 1, i + 1):
                    value[i, q] = value[i, q] - low[i, k] * low[q, k]
            inv[k, k] = root
            for q in range(k):
                inv[k, q] = -root * total([low[k, t] * inv[t, q] for t in range(q, k)])

        def scaled(items):
            return [total([inv[i, k] * items[k] for k in range(i + 1)]) for i in range(8)]

        def solved(items):
            return [total([inv[i, k] * items[i] for i in range(k, 8)]) for k in range(8)]

        rows_s, rows_m = scaled(rows_s), scaled(rows_m)
        done_s, done_m = rows_s[0], rows_m[0]
        for k in range(1, 8):
            done_s = jnp.where(eight == k, rows_s[k], done_s)
            done_m = jnp.where(eight == k, rows_m[k], done_m)
        upper[block] = pltpu.roll(done_s, 8 * block, 1)
        inverse[block] = done_m
        s, m = work[rest], unit[rest]
        columns = [jnp.broadcast_to(s[:, :, k:k + 1], s.shape) for k in range(8)]
        for column, change_s, change_m in zip(columns, solved(rows_s), solved(rows_m)):
            s = s - column * change_s
            m = m - column * change_m
        work[rest] = pltpu.roll(s, n - 8, 2)
        unit[rest] = m

    for part in range(0, tiles, 4):
        pl.loop(part, part + 4)(functools.partial(step, rest=slice(part, tiles)))

    upper[...] = jnp.where(lane >= row, upper[...], 0.0)
    inverse[...] = jnp.where(lane <= row, inverse[...], 0.0)


def factor_kernel(ids_ref, mine_ref, other_ref, parts_ref, r_ref, inv_ref, low_ref, work, unit, upper, inverse):
    tiled, flat = (HALF // 8, 8, HALF), (HALF, HALF)
    first = ids_ref[0] == 0
    for k in range(NX):
        rows = pl.ds(pl.multiple_of(64 * lax.rem(ids_ref[1] + NX - k, NX), 64), 64)
        mine, other = mine_ref[k], other_ref[k]
        r_ref[rows, :HALF] = jnp.where(first, mine, other)
        r_ref[rows, HALF:] = jnp.where(first, other, mine)
    right = r_ref[:, HALF:]
    work[...] = r_ref[:HALF, :HALF].reshape(tiled)
    eliminate(work, unit, upper, inverse)
    r_ref[:HALF, :HALF] = upper[...].reshape(flat)
    inverse_1 = inverse[...].reshape(flat)
    r_ref[HALF:, :HALF] = jnp.zeros(flat, F32)
    cross = dot(inverse_1, right[:HALF], precision=HIGHEST)
    r_ref[:HALF, HALF:] = cross
    work[...] = (right[HALF:] - dot(cross, cross, ((0,), (0,)), HIGHEST)).reshape(tiled)
    lower = dot(cross, inverse_1, ((0,), (0,)), HIGHEST)
    eliminate(work, unit, upper, inverse)
    r_ref[HALF:, HALF:] = upper[...].reshape(flat)
    inverse_2 = inverse[...].reshape(flat)
    below = -dot(inverse_2, lower, precision=HIGHEST)
    zero = jnp.zeros(flat, BF16)
    for start, one, two, three in zip((0, B), split(inverse_1, 2), split(below, 2), split(inverse_2, 2)):
        inv_ref[start:start + HALF, :HALF] = one
        inv_ref[start:start + HALF, HALF:] = zero
        inv_ref[start + HALF:start + B, :HALF] = two
        inv_ref[start + HALF:start + B, HALF:] = three
    basis = dot_split(inv_ref[...], parts_ref[:B], parts_ref[B:])
    low_ref[...] = basis.T.astype(BF16)


def update_kernel(ids_ref, a0_ref, a1_ref, a2_ref, a3_ref, inv_ref, low_ref, trailing_ref, top_ref, updated_ref,
                  sums, held, top, updated, arrived, sent):
    copies = fetches(trailing_ref, held, arrived)
    for k, a_ref in enumerate((a0_ref, a1_ref, a2_ref, a3_ref)):
        sums[pl.ds(pl.multiple_of(64 * lax.rem(ids_ref[1] + NX - k, NX), 64), 64)] = a_ref[...]
    results = []

    def send(source, target, semaphore):
        results.append(pltpu.make_async_copy(source, target, semaphore))
        results[-1].start()

    for tile in range(0, COLS // TILE, WIDE):
        columns = slice(tile * TILE, (tile + WIDE) * TILE)
        rows = dot_split(inv_ref[...], *split(sums[:, columns], 2))
        top[:, columns] = rows
        send(top.at[:, columns], top_ref.at[:, columns], sent.at[0, tile])
        change = dot(low_ref[...], rows.astype(BF16))
        for copy in copies[tile:tile + WIDE]:
            copy.wait()
        updated[:, columns] = (held[:, columns].astype(F32) - change).astype(BF16)
        send(updated.at[:, columns], updated_ref.at[:, columns], sent.at[1, tile])
    for result in results:
        result.wait()


HBM = pl.BlockSpec(memory_space=pltpu.HBM)
VMEM = pl.BlockSpec(memory_space=pltpu.VMEM)
SMEM = pl.BlockSpec(memory_space=pltpu.SMEM)


def cost(flops, size):
    return pl.CostEstimate(flops=int(flops), bytes_accessed=int(size), transcendentals=0)


def limit(mib):
    return pltpu.CompilerParams(vmem_limit_bytes=mib * 2**20)


def array(*shape, dtype=F32):
    return jax.ShapeDtypeStruct(shape, dtype)


def product(ids, mine, other, trailing):
    return pl.pallas_call(
        product_kernel,
        out_shape=(array(2 * B, ROWS, dtype=BF16),) + (array(B // NX, COLS + HALF),) * NX,
        in_specs=[SMEM, VMEM, VMEM, HBM],
        out_specs=(VMEM,) * (1 + NX),
        scratch_shapes=[
            pltpu.VMEM((ROWS, COLS), BF16),
            pltpu.VMEM((B, ROWS), BF16),
            pltpu.VMEM((2, B, 2 * TILE), F32),
            pltpu.VMEM((B, HALF), F32),
            pltpu.SemaphoreType.DMA((COLS // TILE,)),
        ],
        compiler_params=limit(50),
        cost_estimate=cost(3.6e9, 8e6),
    )(ids, mine, other, trailing)


def factor(ids, mine, other, parts):
    return pl.pallas_call(
        factor_kernel,
        out_shape=(array(B, B), array(2 * B, B, dtype=BF16), array(ROWS, B, dtype=BF16)),
        in_specs=[SMEM, VMEM, VMEM, VMEM],
        out_specs=(VMEM,) * 3,
        scratch_shapes=[pltpu.VMEM((HALF // 8, 8, HALF), F32)] * 4,
        compiler_params=limit(20),
        cost_estimate=cost(1.5e10, 3e6),
    )(ids, mine, other, parts)


def update(ids, a, inverse, low, trailing):
    tiles = COLS // TILE
    return pl.pallas_call(
        update_kernel,
        out_shape=(array(B, COLS), array(ROWS, COLS, dtype=BF16)),
        in_specs=[SMEM] + [VMEM] * 6 + [HBM],
        out_specs=(HBM, HBM),
        scratch_shapes=[
            pltpu.VMEM((B, COLS), F32),
            pltpu.VMEM((ROWS, COLS), BF16),
            pltpu.VMEM((B, COLS), F32),
            pltpu.VMEM((ROWS, COLS), BF16),
            pltpu.SemaphoreType.DMA((tiles,)),
            pltpu.SemaphoreType.DMA((2, tiles)),
        ],
        compiler_params=limit(50),
        cost_estimate=cost(3e9, 12e6),
    )(ids, *a, inverse, low, trailing)


def swap_z(block):
    return lax.all_to_all(block, "row", 0, 0, axis_index_groups=Z_GROUPS)


def shift(pieces, axis, routes):
    return [pieces[0]] + [lax.ppermute(pieces[k], axis, routes[k]) for k in range(1, 4)]


def local(panel, trailing):
    row, col = lax.axis_index("row"), lax.axis_index("col")
    ids = jnp.stack([col % 2, row // NZ, col // 2]).astype(jnp.int32)
    with jax.named_scope("gather_panel"):
        mine = jnp.stack(shift([panel.T] * 4, "col", Y_ROUTES))
        other = lax.ppermute(mine, "col", SIBLING)
    with jax.named_scope("product"):
        parts, *pieces = product(ids, mine, other, trailing)
    with jax.named_scope("sum_x"):
        sums = sum(shift(pieces, "row", X_ROUTES))
    with jax.named_scope("sum_z"):
        sums = jnp.sum(swap_z(sums.reshape(NZ, 8, COLS + HALF)), axis=0)
    with jax.named_scope("gather_z"):
        sums = swap_z(jnp.broadcast_to(sums[None], (NZ, 8, COLS + HALF))).reshape(64, COLS + HALF)
    with jax.named_scope("gather_gram"):
        gram_mine = jnp.stack(shift([sums[:, COLS:]] * NX, "row", X_ROUTES))
        gram_other = lax.ppermute(gram_mine, "col", SIBLING)
    with jax.named_scope("gather_x"):
        blocks = shift([sums[:, :COLS]] * NX, "row", X_ROUTES)
    with jax.named_scope("factor"):
        r_factor, inverse, low = factor(ids, gram_mine, gram_other, parts)
    with jax.named_scope("update"):
        top, updated = update(ids, blocks, inverse, low, trailing)
    return r_factor, top, updated


def solution(mesh):
    return jax.shard_map(
        local,
        mesh=mesh,
        in_specs=(P("row", "col"), P("row", "col")),
        out_specs=(P(), P(None, "col"), P("row", "col")),
        check_vma=False,
    )
```

```python
import functools

import jax
import jax.numpy as jnp
from jax import lax
from jax.experimental import pallas as pl
from jax.experimental.pallas import tpu as pltpu
from jax.sharding import PartitionSpec as P

F32 = jnp.float32
BF16 = jnp.bfloat16
HIGHEST = lax.Precision.HIGHEST
NX, NZ = 4, 8
B, ROWS, COLS, HALF, TILE = 256, 1024, 2048, 128, 256
WIDE = 4

Z_GROUPS = [[x * NZ + z for z in range(NZ)] for x in range(NX)]
SIBLING = [(c, c ^ 1) for c in range(8)]
Y_ROUTES = [[(c, (c + 2 * k) % 8) for c in range(8)] for k in range(4)]
X_ROUTES = [[(x * NZ + z, (x + k) % NX * NZ + z) for x in range(NX) for z in range(NZ)] for k in range(NX)]


def dot(a, b, contract=((1,), (0,)), precision=None):
    return lax.dot_general(a, b, (contract, ((), ())), precision=precision, preferred_element_type=F32)


def split(value, count):
    terms = []
    for _ in range(count):
        terms.append(value.astype(BF16))
        value = value - terms[-1].astype(F32)
    return terms


def dot_split(left, high, low):
    rows = left.shape[0] // 2
    both = dot(left, high)
    return both[rows:] + dot(left[:rows], low) + both[:rows]


def tile_of(index):
    return slice(index * TILE, index * TILE + TILE)


def fetches(source_ref, target_ref, arrived):
    copies = [
        pltpu.make_async_copy(source_ref.at[:, tile_of(tile)], target_ref.at[:, tile_of(tile)], arrived.at[tile])
        for tile in range(COLS // TILE)
    ]
    for copy in copies:
        copy.start()
    return copies


def product_kernel(ids_ref, *refs):
    mine, other, trailing_ref, parts_ref, pieces = refs[:4], refs[4:8], refs[8], refs[9], refs[10:10 + NX]
    held, third, whole, gram, arrived = refs[10 + NX:]
    copies = fetches(trailing_ref, held, arrived)
    core, x, y = ids_ref[0], ids_ref[1], ids_ref[2]
    for k in range(4):
        for ref, offset in ((mine[k], 32 * core), (other[k], 32 - 32 * core)):
            start = 64 * lax.rem(y + 4 - k, 4) + offset
            high, middle, low = split(ref[...], 3)
            parts_ref[pl.ds(pl.multiple_of(start, 32), 32)] = high
            parts_ref[pl.ds(pl.multiple_of(B + start, 32), 32)] = middle
            third[pl.ds(pl.multiple_of(start, 32), 32)] = low
    half = pl.multiple_of(core * HALF, HALF)
    last = ((1,), (1,))
    one = dot(parts_ref[...], parts_ref[pl.ds(half, HALF)], last)
    two = dot(parts_ref[...], parts_ref[pl.ds(pl.multiple_of(B + half, HALF), HALF)], last)
    small = dot(third[...], parts_ref[pl.ds(half, HALF)], last) + dot(parts_ref[:B], third[pl.ds(half, HALF)], last)
    gram[...] = small + two[B:] + one[B:] + two[:B] + one[:B]

    def hand_out(source, columns):
        for k in range(NX):
            start = pl.multiple_of(64 * lax.rem(x + k, NX), 64)
            pieces[k][:, columns] = source[pl.ds(start, 64)]

    hand_out(gram, slice(COLS, COLS + HALF))
    for tile in range(0, COLS // TILE, 2):
        for copy in copies[tile:tile + 2]:
            copy.wait()
        columns = slice(tile * TILE, (tile + 2) * TILE)
        both = dot(parts_ref[...], held[:, columns])
        slot = whole.at[tile // 2 % 2]
        slot[...] = both[B:] + both[:B]
        hand_out(slot, columns)


def eliminate(work, unit, upper, inverse):
    n, tiles = HALF, HALF // 8
    shape = (tiles, 8, n)
    row = 8 * lax.broadcasted_iota(jnp.int32, shape, 0) + lax.broadcasted_iota(jnp.int32, shape, 1)
    lane = lax.broadcasted_iota(jnp.int32, shape, 2)
    eight = lax.broadcasted_iota(jnp.int32, (8, n), 0)
    unit[...] = (lane == row).astype(F32)

    def reciprocal_root(value):
        guess = lax.rsqrt(value)
        return guess * (1.5 - 0.5 * value * guess * guess)

    def total(terms):
        while len(terms) > 1:
            terms = [sum(terms[at:at + 2]) for at in range(0, len(terms), 2)]
        return terms[0]

    def step(block, rest):
        pivot_s, pivot_m = work[block], unit[block]
        rows_s = [jnp.broadcast_to(pivot_s[k:k + 1], (8, n)) for k in range(8)]
        rows_m = [jnp.broadcast_to(pivot_m[k:k + 1], (8, n)) for k in range(8)]
        value = {(i, k): jnp.broadcast_to(pivot_s[i:i + 1, k:k + 1], (8, n)) for i in range(8) for k in range(i + 1)}
        low, inv = {}, {}
        for k in range(8):
            root = reciprocal_root(value[k, k])
            for i in range(k + 1, 8):
                low[i, k] = value[i, k] * root
            for i in range(k + 1, 8):
                for q in range(k + 1, i + 1):
                    value[i, q] = value[i, q] - low[i, k] * low[q, k]
            inv[k, k] = root
            for q in range(k):
                inv[k, q] = -root * total([low[k, t] * inv[t, q] for t in range(q, k)])

        def scaled(items):
            return [total([inv[i, k] * items[k] for k in range(i + 1)]) for i in range(8)]

        def solved(items):
            return [total([inv[i, k] * items[i] for i in range(k, 8)]) for k in range(8)]

        rows_s, rows_m = scaled(rows_s), scaled(rows_m)
        done_s, done_m = rows_s[0], rows_m[0]
        for k in range(1, 8):
            done_s = jnp.where(eight == k, rows_s[k], done_s)
            done_m = jnp.where(eight == k, rows_m[k], done_m)
        upper[block] = pltpu.roll(done_s, 8 * block, 1)
        inverse[block] = done_m
        s, m = work[rest], unit[rest]
        columns = [jnp.broadcast_to(s[:, :, k:k + 1], s.shape) for k in range(8)]
        for column, change_s, change_m in zip(columns, solved(rows_s), solved(rows_m)):
            s = s - column * change_s
            m = m - column * change_m
        work[rest] = pltpu.roll(s, n - 8, 2)
        unit[rest] = m

    for part in range(0, tiles, 4):
        pl.loop(part, part + 4)(functools.partial(step, rest=slice(part, tiles)))

    upper[...] = jnp.where(lane >= row, upper[...], 0.0)
    inverse[...] = jnp.where(lane <= row, inverse[...], 0.0)


def factor_kernel(ids_ref, mine_ref, other_ref, parts_ref, trailing_ref, r_ref, inv_ref, low_ref, copy_ref,
                  work, unit, upper, inverse, arrived):
    fetch = pltpu.make_async_copy(trailing_ref, copy_ref, arrived)
    fetch.start()
    tiled, flat = (HALF // 8, 8, HALF), (HALF, HALF)
    first = ids_ref[0] == 0
    for k in range(NX):
        rows = pl.ds(pl.multiple_of(64 * lax.rem(ids_ref[1] + NX - k, NX), 64), 64)
        mine, other = mine_ref[k], other_ref[k]
        r_ref[rows, :HALF] = jnp.where(first, mine, other)
        r_ref[rows, HALF:] = jnp.where(first, other, mine)
    right = r_ref[:, HALF:]
    work[...] = r_ref[:HALF, :HALF].reshape(tiled)
    eliminate(work, unit, upper, inverse)
    r_ref[:HALF, :HALF] = upper[...].reshape(flat)
    inverse_1 = inverse[...].reshape(flat)
    r_ref[HALF:, :HALF] = jnp.zeros(flat, F32)
    cross = dot(inverse_1, right[:HALF], precision=HIGHEST)
    r_ref[:HALF, HALF:] = cross
    work[...] = (right[HALF:] - dot(cross, cross, ((0,), (0,)), HIGHEST)).reshape(tiled)
    lower = dot(cross, inverse_1, ((0,), (0,)), HIGHEST)
    eliminate(work, unit, upper, inverse)
    r_ref[HALF:, HALF:] = upper[...].reshape(flat)
    inverse_2 = inverse[...].reshape(flat)
    below = -dot(inverse_2, lower, precision=HIGHEST)
    zero = jnp.zeros(flat, BF16)
    for start, one, two, three in zip((0, B), split(inverse_1, 2), split(below, 2), split(inverse_2, 2)):
        inv_ref[start:start + HALF, :HALF] = one
        inv_ref[start:start + HALF, HALF:] = zero
        inv_ref[start + HALF:start + B, :HALF] = two
        inv_ref[start + HALF:start + B, HALF:] = three
    basis = dot_split(inv_ref[...], parts_ref[:B], parts_ref[B:])
    low_ref[...] = basis.T.astype(BF16)
    fetch.wait()


def update_kernel(ids_ref, a0_ref, a1_ref, a2_ref, a3_ref, inv_ref, low_ref, trailing_ref, top_ref, updated_ref,
                  sums, top, updated, sent):
    for k, a_ref in enumerate((a0_ref, a1_ref, a2_ref, a3_ref)):
        sums[pl.ds(pl.multiple_of(64 * lax.rem(ids_ref[1] + NX - k, NX), 64), 64)] = a_ref[...]
    results = []

    def send(source, target, semaphore):
        results.append(pltpu.make_async_copy(source, target, semaphore))
        results[-1].start()

    for tile in range(0, COLS // TILE, WIDE):
        columns = slice(tile * TILE, (tile + WIDE) * TILE)
        rows = dot_split(inv_ref[...], *split(sums[:, columns], 2))
        top[:, columns] = rows
        send(top.at[:, columns], top_ref.at[:, columns], sent.at[0, tile])
        change = dot(low_ref[...], rows.astype(BF16))
        updated[:, columns] = (trailing_ref[:, columns].astype(F32) - change).astype(BF16)
        send(updated.at[:, columns], updated_ref.at[:, columns], sent.at[1, tile])
    for result in results:
        result.wait()


HBM = pl.BlockSpec(memory_space=pltpu.HBM)
VMEM = pl.BlockSpec(memory_space=pltpu.VMEM)
SMEM = pl.BlockSpec(memory_space=pltpu.SMEM)


def cost(flops, size):
    return pl.CostEstimate(flops=int(flops), bytes_accessed=int(size), transcendentals=0)


def limit(mib):
    return pltpu.CompilerParams(vmem_limit_bytes=mib * 2**20)


def array(*shape, dtype=F32):
    return jax.ShapeDtypeStruct(shape, dtype)


def product(ids, mine, other, trailing):
    return pl.pallas_call(
        product_kernel,
        out_shape=(array(2 * B, ROWS, dtype=BF16),) + (array(B // NX, COLS + HALF),) * NX,
        in_specs=[SMEM] + [VMEM] * 8 + [HBM],
        out_specs=(VMEM,) * (1 + NX),
        scratch_shapes=[
            pltpu.VMEM((ROWS, COLS), BF16),
            pltpu.VMEM((B, ROWS), BF16),
            pltpu.VMEM((2, B, 2 * TILE), F32),
            pltpu.VMEM((B, HALF), F32),
            pltpu.SemaphoreType.DMA((COLS // TILE,)),
        ],
        compiler_params=limit(50),
        cost_estimate=cost(3.6e9, 8e6),
    )(ids, *mine, *other, trailing)


def factor(ids, mine, other, parts, trailing):
    return pl.pallas_call(
        factor_kernel,
        out_shape=(
            array(B, B),
            array(2 * B, B, dtype=BF16),
            array(ROWS, B, dtype=BF16),
            array(ROWS, COLS, dtype=BF16),
        ),
        in_specs=[SMEM, VMEM, VMEM, VMEM, HBM],
        out_specs=(VMEM,) * 4,
        scratch_shapes=[pltpu.VMEM((HALF // 8, 8, HALF), F32)] * 4 + [pltpu.SemaphoreType.DMA],
        compiler_params=limit(45),
        cost_estimate=cost(1e6, 1e3),
    )(ids, mine, other, parts, trailing)


def update(ids, a, inverse, low, trailing):
    tiles = COLS // TILE
    return pl.pallas_call(
        update_kernel,
        out_shape=(array(B, COLS), array(ROWS, COLS, dtype=BF16)),
        in_specs=[SMEM] + [VMEM] * 7,
        out_specs=(HBM, HBM),
        scratch_shapes=[
            pltpu.VMEM((B, COLS), F32),
            pltpu.VMEM((B, COLS), F32),
            pltpu.VMEM((ROWS, COLS), BF16),
            pltpu.SemaphoreType.DMA((2, tiles)),
        ],
        compiler_params=limit(36),
        cost_estimate=cost(3e9, 12e6),
    )(ids, *a, inverse, low, trailing)


def swap_z(block):
    return lax.all_to_all(block, "row", 0, 0, axis_index_groups=Z_GROUPS)


def shift(pieces, axis, routes):
    return [pieces[0]] + [lax.ppermute(pieces[k], axis, routes[k]) for k in range(1, 4)]


def local(panel, trailing):
    row, col = lax.axis_index("row"), lax.axis_index("col")
    ids = jnp.stack([col % 2, row // NZ, col // 2]).astype(jnp.int32)
    with jax.named_scope("gather_panel"):
        mine = shift([panel.T] * 4, "col", Y_ROUTES)
        other = [lax.ppermute(piece, "col", SIBLING) for piece in mine]
    with jax.named_scope("product"):
        parts, *pieces = product(ids, mine, other, trailing)
    with jax.named_scope("sum_x"):
        sums = sum(shift(pieces, "row", X_ROUTES))
    with jax.named_scope("sum_z"):
        sums = jnp.sum(swap_z(sums.reshape(NZ, 8, COLS + HALF)), axis=0)
    with jax.named_scope("gather_z"):
        sums = swap_z(jnp.broadcast_to(sums[None], (NZ, 8, COLS + HALF))).reshape(64, COLS + HALF)
    with jax.named_scope("gather_gram"):
        gram_mine = jnp.stack(shift([sums[:, COLS:]] * NX, "row", X_ROUTES))
        gram_other = lax.ppermute(gram_mine, "col", SIBLING)
    with jax.named_scope("gather_x"):
        blocks = shift([sums[:, :COLS]] * NX, "row", X_ROUTES)
    with jax.named_scope("factor"):
        r_factor, inverse, low, trailing = factor(ids, gram_mine, gram_other, parts, trailing)
    with jax.named_scope("update"):
        top, updated = update(ids, blocks, inverse, low, trailing)
    return r_factor, top, updated


def solution(mesh):
    return jax.shard_map(
        local,
        mesh=mesh,
        in_specs=(P("row", "col"), P("row", "col")),
        out_specs=(P(), P(None, "col"), P("row", "col")),
        check_vma=False,
    )
```

```python
import functools

import jax
import jax.numpy as jnp
from jax import lax
from jax.experimental import pallas as pl
from jax.experimental.pallas import tpu as pltpu
from jax.sharding import PartitionSpec as P

F32 = jnp.float32
BF16 = jnp.bfloat16
HIGHEST = lax.Precision.HIGHEST
NX, NZ = 4, 8
B, ROWS, COLS, HALF, TILE = 256, 1024, 2048, 128, 256
WIDE = 4

Z_GROUPS = [[x * NZ + z for z in range(NZ)] for x in range(NX)]
SIBLING = [(c, c ^ 1) for c in range(8)]
Y_ROUTES = [[(c, (c + 2 * k) % 8) for c in range(8)] for k in range(4)]
X_ROUTES = [[(x * NZ + z, (x + k) % NX * NZ + z) for x in range(NX) for z in range(NZ)] for k in range(NX)]


def dot(a, b, contract=((1,), (0,)), precision=None):
    return lax.dot_general(a, b, (contract, ((), ())), precision=precision, preferred_element_type=F32)


def split(value, count):
    terms = []
    for _ in range(count):
        terms.append(value.astype(BF16))
        value = value - terms[-1].astype(F32)
    return terms


def dot_split(left, high, low):
    rows = left.shape[0] // 2
    both = dot(left, high)
    return both[rows:] + dot(left[:rows], low) + both[:rows]


def tile_of(index):
    return slice(index * TILE, index * TILE + TILE)


def fetches(source_ref, target_ref, arrived):
    copies = [
        pltpu.make_async_copy(source_ref.at[:, tile_of(tile)], target_ref.at[:, tile_of(tile)], arrived.at[tile])
        for tile in range(COLS // TILE)
    ]
    for copy in copies:
        copy.start()
    return copies


def product_kernel(ids_ref, *refs):
    mine, other, trailing_ref, parts_ref, pieces = refs[:4], refs[4:8], refs[8], refs[9], refs[10:10 + NX]
    held, third, whole, gram, arrived = refs[10 + NX:]
    copies = fetches(trailing_ref, held, arrived)
    core, x, y = ids_ref[0], ids_ref[1], ids_ref[2]
    for k in range(4):
        for ref, offset in ((mine[k], 32 * core), (other[k], 32 - 32 * core)):
            start = 64 * lax.rem(y + 4 - k, 4) + offset
            high, middle, low = split(ref[...], 3)
            parts_ref[pl.ds(pl.multiple_of(start, 32), 32)] = high
            parts_ref[pl.ds(pl.multiple_of(B + start, 32), 32)] = middle
            third[pl.ds(pl.multiple_of(start, 32), 32)] = low
    half = pl.multiple_of(core * HALF, HALF)
    last = ((1,), (1,))
    one = dot(parts_ref[...], parts_ref[pl.ds(half, HALF)], last)
    two = dot(parts_ref[...], parts_ref[pl.ds(pl.multiple_of(B + half, HALF), HALF)], last)
    small = dot(third[...], parts_ref[pl.ds(half, HALF)], last) + dot(parts_ref[:B], third[pl.ds(half, HALF)], last)
    gram[...] = small + two[B:] + one[B:] + two[:B] + one[:B]

    def hand_out(source, columns):
        for k in range(NX):
            start = pl.multiple_of(64 * lax.rem(x + k, NX), 64)
            pieces[k][:, columns] = source[pl.ds(start, 64)]

    hand_out(gram, slice(COLS, COLS + HALF))
    for tile in range(0, COLS // TILE, 2):
        for copy in copies[tile:tile + 2]:
            copy.wait()
        columns = slice(tile * TILE, (tile + 2) * TILE)
        both = dot(parts_ref[...], held[:, columns])
        slot = whole.at[tile // 2 % 2]
        slot[...] = both[B:] + both[:B]
        hand_out(slot, columns)


def eliminate(work, unit, upper, inverse):
    n, tiles = HALF, HALF // 8
    shape = (tiles, 8, n)
    row = 8 * lax.broadcasted_iota(jnp.int32, shape, 0) + lax.broadcasted_iota(jnp.int32, shape, 1)
    lane = lax.broadcasted_iota(jnp.int32, shape, 2)
    eight = lax.broadcasted_iota(jnp.int32, (8, n), 0)
    unit[...] = (lane == row).astype(F32)

    def reciprocal_root(value):
        guess = lax.rsqrt(value)
        return guess * (1.5 - 0.5 * value * guess * guess)

    def total(terms):
        while len(terms) > 1:
            terms = [sum(terms[at:at + 2]) for at in range(0, len(terms), 2)]
        return terms[0]

    def step(block, rest):
        pivot_s, pivot_m = work[block], unit[block]
        rows_s = [jnp.broadcast_to(pivot_s[k:k + 1], (8, n)) for k in range(8)]
        rows_m = [jnp.broadcast_to(pivot_m[k:k + 1], (8, n)) for k in range(8)]
        value = {(i, k): jnp.broadcast_to(pivot_s[i:i + 1, k:k + 1], (8, n)) for i in range(8) for k in range(i + 1)}
        low, inv = {}, {}
        for k in range(8):
            root = reciprocal_root(value[k, k])
            for i in range(k + 1, 8):
                low[i, k] = value[i, k] * root
            for i in range(k + 1, 8):
                for q in range(k + 1, i + 1):
                    value[i, q] = value[i, q] - low[i, k] * low[q, k]
            inv[k, k] = root
            for q in range(k):
                inv[k, q] = -root * total([low[k, t] * inv[t, q] for t in range(q, k)])

        def scaled(items):
            return [total([inv[i, k] * items[k] for k in range(i + 1)]) for i in range(8)]

        def solved(items):
            return [total([inv[i, k] * items[i] for i in range(k, 8)]) for k in range(8)]

        rows_s, rows_m = scaled(rows_s), scaled(rows_m)
        done_s, done_m = rows_s[0], rows_m[0]
        for k in range(1, 8):
            done_s = jnp.where(eight == k, rows_s[k], done_s)
            done_m = jnp.where(eight == k, rows_m[k], done_m)
        upper[block] = pltpu.roll(done_s, 8 * block, 1)
        inverse[block] = done_m
        s, m = work[rest], unit[rest]
        columns = [jnp.broadcast_to(s[:, :, k:k + 1], s.shape) for k in range(8)]
        for column, change_s, change_m in zip(columns, solved(rows_s), solved(rows_m)):
            s = s - column * change_s
            m = m - column * change_m
        work[rest] = pltpu.roll(s, n - 8, 2)
        unit[rest] = m

    for part in range(0, tiles, 4):
        pl.loop(part, part + 4)(functools.partial(step, rest=slice(part, tiles)))

    upper[...] = jnp.where(lane >= row, upper[...], 0.0)
    inverse[...] = jnp.where(lane <= row, inverse[...], 0.0)


def factor_kernel(ids_ref, mine_ref, other_ref, parts_ref, trailing_ref, r_ref, inv_ref, low_ref, copy_ref,
                  work, unit, upper, inverse, arrived):
    fetch = pltpu.make_async_copy(trailing_ref, copy_ref, arrived)
    fetch.start()
    tiled, flat = (HALF // 8, 8, HALF), (HALF, HALF)
    first = ids_ref[0] == 0
    for k in range(NX):
        rows = pl.ds(pl.multiple_of(64 * lax.rem(ids_ref[1] + NX - k, NX), 64), 64)
        mine, other = mine_ref[k], other_ref[k]
        r_ref[rows, :HALF] = jnp.where(first, mine, other)
        r_ref[rows, HALF:] = jnp.where(first, other, mine)
    right = r_ref[:, HALF:]
    work[...] = r_ref[:HALF, :HALF].reshape(tiled)
    eliminate(work, unit, upper, inverse)
    r_ref[:HALF, :HALF] = upper[...].reshape(flat)
    inverse_1 = inverse[...].reshape(flat)
    r_ref[HALF:, :HALF] = jnp.zeros(flat, F32)
    cross = dot(inverse_1, right[:HALF], precision=HIGHEST)
    r_ref[:HALF, HALF:] = cross
    work[...] = (right[HALF:] - dot(cross, cross, ((0,), (0,)), HIGHEST)).reshape(tiled)
    lower = dot(cross, inverse_1, ((0,), (0,)), HIGHEST)
    eliminate(work, unit, upper, inverse)
    r_ref[HALF:, HALF:] = upper[...].reshape(flat)
    inverse_2 = inverse[...].reshape(flat)
    below = -dot(inverse_2, lower, precision=HIGHEST)
    zero = jnp.zeros(flat, BF16)
    for start, one, two, three in zip((0, B), split(inverse_1, 2), split(below, 2), split(inverse_2, 2)):
        inv_ref[start:start + HALF, :HALF] = one
        inv_ref[start:start + HALF, HALF:] = zero
        inv_ref[start + HALF:start + B, :HALF] = two
        inv_ref[start + HALF:start + B, HALF:] = three
    basis = dot_split(inv_ref[...], parts_ref[:B], parts_ref[B:])
    low_ref[...] = basis.T.astype(BF16)
    fetch.wait()


def update_kernel(ids_ref, a0_ref, a1_ref, a2_ref, a3_ref, inv_ref, low_ref, trailing_ref, top_ref, updated_ref,
                  sums, top, updated, sent):
    for k, a_ref in enumerate((a0_ref, a1_ref, a2_ref, a3_ref)):
        sums[pl.ds(pl.multiple_of(64 * lax.rem(ids_ref[1] + NX - k, NX), 64), 64)] = a_ref[...]
    results = []

    def send(source, target, semaphore):
        results.append(pltpu.make_async_copy(source, target, semaphore))
        results[-1].start()

    for tile in range(0, COLS // TILE, WIDE):
        columns = slice(tile * TILE, (tile + WIDE) * TILE)
        rows = dot_split(inv_ref[...], *split(sums[:, columns], 2))
        top[:, columns] = rows
        send(top.at[:, columns], top_ref.at[:, columns], sent.at[0, tile])
        change = dot(low_ref[...], rows.astype(BF16))
        updated[:, columns] = (trailing_ref[:, columns].astype(F32) - change).astype(BF16)
        send(updated.at[:, columns], updated_ref.at[:, columns], sent.at[1, tile])
    for result in results:
        result.wait()


HBM = pl.BlockSpec(memory_space=pltpu.HBM)
VMEM = pl.BlockSpec(memory_space=pltpu.VMEM)
SMEM = pl.BlockSpec(memory_space=pltpu.SMEM)


def cost(flops, size):
    return pl.CostEstimate(flops=int(flops), bytes_accessed=int(size), transcendentals=0)


def limit(mib):
    return pltpu.CompilerParams(vmem_limit_bytes=mib * 2**20)


def array(*shape, dtype=F32):
    return jax.ShapeDtypeStruct(shape, dtype)


def product(ids, mine, other, trailing):
    return pl.pallas_call(
        product_kernel,
        out_shape=(array(2 * B, ROWS, dtype=BF16),) + (array(B // NX, COLS + HALF),) * NX,
        in_specs=[SMEM] + [VMEM] * 8 + [HBM],
        out_specs=(VMEM,) * (1 + NX),
        scratch_shapes=[
            pltpu.VMEM((ROWS, COLS), BF16),
            pltpu.VMEM((B, ROWS), BF16),
            pltpu.VMEM((2, B, 2 * TILE), F32),
            pltpu.VMEM((B, HALF), F32),
            pltpu.SemaphoreType.DMA((COLS // TILE,)),
        ],
        compiler_params=limit(50),
        cost_estimate=cost(3.6e9, 8e6),
    )(ids, *mine, *other, trailing)


def factor(ids, mine, other, parts, trailing):
    return pl.pallas_call(
        factor_kernel,
        out_shape=(
            array(B, B),
            array(2 * B, B, dtype=BF16),
            array(ROWS, B, dtype=BF16),
            array(ROWS, COLS, dtype=BF16),
        ),
        in_specs=[SMEM, VMEM, VMEM, VMEM, HBM],
        out_specs=(VMEM,) * 4,
        scratch_shapes=[pltpu.VMEM((HALF // 8, 8, HALF), F32)] * 4 + [pltpu.SemaphoreType.DMA],
        compiler_params=limit(45),
        cost_estimate=cost(3.5e9, 1e3),
    )(ids, mine, other, parts, trailing)


def update(ids, a, inverse, low, trailing):
    tiles = COLS // TILE
    return pl.pallas_call(
        update_kernel,
        out_shape=(array(B, COLS), array(ROWS, COLS, dtype=BF16)),
        in_specs=[SMEM] + [VMEM] * 7,
        out_specs=(HBM, HBM),
        scratch_shapes=[
            pltpu.VMEM((B, COLS), F32),
            pltpu.VMEM((B, COLS), F32),
            pltpu.VMEM((ROWS, COLS), BF16),
            pltpu.SemaphoreType.DMA((2, tiles)),
        ],
        compiler_params=limit(36),
        cost_estimate=cost(3e9, 12e6),
    )(ids, *a, inverse, low, trailing)


def swap_z(block):
    return lax.all_to_all(block, "row", 0, 0, axis_index_groups=Z_GROUPS)


def shift(pieces, axis, routes):
    return [pieces[0]] + [lax.ppermute(pieces[k], axis, routes[k]) for k in range(1, 4)]


def local(panel, trailing):
    row, col = lax.axis_index("row"), lax.axis_index("col")
    ids = jnp.stack([col % 2, row // NZ, col // 2]).astype(jnp.int32)
    with jax.named_scope("gather_panel"):
        mine = shift([panel.T] * 4, "col", Y_ROUTES)
        other = [lax.ppermute(piece, "col", SIBLING) for piece in mine]
    with jax.named_scope("product"):
        parts, *pieces = product(ids, mine, other, trailing)
    with jax.named_scope("sum_x"):
        sums = sum(shift(pieces, "row", X_ROUTES))
    with jax.named_scope("sum_z"):
        sums = jnp.sum(swap_z(sums.reshape(NZ, 8, COLS + HALF)), axis=0)
    with jax.named_scope("gather_z"):
        sums = swap_z(jnp.broadcast_to(sums[None], (NZ, 8, COLS + HALF))).reshape(64, COLS + HALF)
    with jax.named_scope("gather_gram"):
        gram_mine = jnp.stack(shift([sums[:, COLS:]] * NX, "row", X_ROUTES))
        gram_other = lax.ppermute(gram_mine, "col", SIBLING)
    with jax.named_scope("gather_x"):
        blocks = shift([sums[:, :COLS]] * NX, "row", X_ROUTES)
    with jax.named_scope("factor"):
        r_factor, inverse, low, trailing = factor(ids, gram_mine, gram_other, parts, trailing)
    with jax.named_scope("update"):
        top, updated = update(ids, blocks, inverse, low, trailing)
    return r_factor, top, updated


def solution(mesh):
    return jax.shard_map(
        local,
        mesh=mesh,
        in_specs=(P("row", "col"), P("row", "col")),
        out_specs=(P(), P(None, "col"), P("row", "col")),
        check_vma=False,
    )
```

```python
import functools

import jax
import jax.numpy as jnp
from jax import lax
from jax.experimental import pallas as pl
from jax.experimental.pallas import tpu as pltpu
from jax.sharding import PartitionSpec as P

F32 = jnp.float32
BF16 = jnp.bfloat16
HIGHEST = lax.Precision.HIGHEST
NX, NZ = 4, 8
B, ROWS, COLS, HALF, TILE = 256, 1024, 2048, 128, 256
WIDE = 4

Z_GROUPS = [[x * NZ + z for z in range(NZ)] for x in range(NX)]
SIBLING = [(c, c ^ 1) for c in range(8)]
Y_ROUTES = [[(c, (c + 2 * k) % 8) for c in range(8)] for k in range(4)]
X_ROUTES = [[(x * NZ + z, (x + k) % NX * NZ + z) for x in range(NX) for z in range(NZ)] for k in range(NX)]


def dot(a, b, contract=((1,), (0,)), precision=None):
    return lax.dot_general(a, b, (contract, ((), ())), precision=precision, preferred_element_type=F32)


def split(value, count):
    terms = []
    for _ in range(count):
        terms.append(value.astype(BF16))
        value = value - terms[-1].astype(F32)
    return terms


def dot_split(left, high, low):
    rows = left.shape[0] // 2
    both = dot(left, high)
    return both[rows:] + dot(left[:rows], low) + both[:rows]


def tile_of(index):
    return slice(index * TILE, index * TILE + TILE)


def fetches(source_ref, target_ref, arrived):
    copies = [
        pltpu.make_async_copy(source_ref.at[:, tile_of(tile)], target_ref.at[:, tile_of(tile)], arrived.at[tile])
        for tile in range(COLS // TILE)
    ]
    for copy in copies:
        copy.start()
    return copies


def product_kernel(ids_ref, *refs):
    mine, other, trailing_ref, parts_ref, pieces = refs[:4], refs[4:8], refs[8], refs[9], refs[10:10 + NX]
    held, third, whole, gram, arrived = refs[10 + NX:]
    copies = fetches(trailing_ref, held, arrived)
    core, x, y = ids_ref[0], ids_ref[1], ids_ref[2]
    for k in range(4):
        for ref, offset in ((mine[k], 32 * core), (other[k], 32 - 32 * core)):
            start = 64 * lax.rem(y + 4 - k, 4) + offset
            high, middle, low = split(ref[...], 3)
            parts_ref[pl.ds(pl.multiple_of(start, 32), 32)] = high
            parts_ref[pl.ds(pl.multiple_of(B + start, 32), 32)] = middle
            third[pl.ds(pl.multiple_of(start, 32), 32)] = low
    half = pl.multiple_of(core * HALF, HALF)
    last = ((1,), (1,))
    one = dot(parts_ref[...], parts_ref[pl.ds(half, HALF)], last)
    two = dot(parts_ref[...], parts_ref[pl.ds(pl.multiple_of(B + half, HALF), HALF)], last)
    small = dot(third[...], parts_ref[pl.ds(half, HALF)], last) + dot(parts_ref[:B], third[pl.ds(half, HALF)], last)
    gram[...] = small + two[B:] + one[B:] + two[:B] + one[:B]

    def hand_out(source, columns):
        for k in range(NX):
            start = pl.multiple_of(64 * lax.rem(x + k, NX), 64)
            pieces[k][:, columns] = source[pl.ds(start, 64)]

    hand_out(gram, slice(COLS, COLS + HALF))
    for tile in range(0, COLS // TILE, 2):
        for copy in copies[tile:tile + 2]:
            copy.wait()
        columns = slice(tile * TILE, (tile + 2) * TILE)
        both = dot(parts_ref[...], held[:, columns])
        slot = whole.at[tile // 2 % 2]
        slot[...] = both[B:] + both[:B]
        hand_out(slot, columns)


def blocks_of(ref):
    return [(slice(r, r + 16), slice(c, c + HALF)) for r in range(0, 64, 16) for c in range(0, ref.shape[1], HALF)]


def add_kernel(p0_ref, p1_ref, p2_ref, p3_ref, *outs):
    for out, place in zip(outs, blocks_of(p0_ref)):
        out[...] = p0_ref[place] + p1_ref[place] + (p2_ref[place] + p3_ref[place])


def join_kernel(*refs):
    blocks, sums_ref, gram_ref = refs[:-2], refs[-2], refs[-1]
    count = (COLS + HALF) // HALF
    for at, block in enumerate(blocks):
        row, column = divmod(at, count)
        rows = slice(16 * row, 16 * row + 16)
        if column < count - 1:
            sums_ref[rows, column * HALF:column * HALF + HALF] = block[...]
        else:
            gram_ref[rows] = block[...]


def eliminate(work, unit, upper, inverse):
    n, tiles = HALF, HALF // 8
    shape = (tiles, 8, n)
    row = 8 * lax.broadcasted_iota(jnp.int32, shape, 0) + lax.broadcasted_iota(jnp.int32, shape, 1)
    lane = lax.broadcasted_iota(jnp.int32, shape, 2)
    eight = lax.broadcasted_iota(jnp.int32, (8, n), 0)
    unit[...] = (lane == row).astype(F32)

    def reciprocal_root(value):
        guess = lax.rsqrt(value)
        return guess * (1.5 - 0.5 * value * guess * guess)

    def total(terms):
        while len(terms) > 1:
            terms = [sum(terms[at:at + 2]) for at in range(0, len(terms), 2)]
        return terms[0]

    def step(block, rest):
        pivot_s, pivot_m = work[block], unit[block]
        rows_s = [jnp.broadcast_to(pivot_s[k:k + 1], (8, n)) for k in range(8)]
        rows_m = [jnp.broadcast_to(pivot_m[k:k + 1], (8, n)) for k in range(8)]
        value = {(i, k): jnp.broadcast_to(pivot_s[i:i + 1, k:k + 1], (8, n)) for i in range(8) for k in range(i + 1)}
        low, inv = {}, {}
        for k in range(8):
            root = reciprocal_root(value[k, k])
            for i in range(k + 1, 8):
                low[i, k] = value[i, k] * root
            for i in range(k + 1, 8):
                for q in range(k + 1, i + 1):
                    value[i, q] = value[i, q] - low[i, k] * low[q, k]
            inv[k, k] = root
            for q in range(k):
                inv[k, q] = -root * total([low[k, t] * inv[t, q] for t in range(q, k)])

        def scaled(items):
            return [total([inv[i, k] * items[k] for k in range(i + 1)]) for i in range(8)]

        def solved(items):
            return [total([inv[i, k] * items[i] for i in range(k, 8)]) for k in range(8)]

        rows_s, rows_m = scaled(rows_s), scaled(rows_m)
        done_s, done_m = rows_s[0], rows_m[0]
        for k in range(1, 8):
            done_s = jnp.where(eight == k, rows_s[k], done_s)
            done_m = jnp.where(eight == k, rows_m[k], done_m)
        upper[block] = pltpu.roll(done_s, 8 * block, 1)
        inverse[block] = done_m
        s, m = work[rest], unit[rest]
        columns = [jnp.broadcast_to(s[:, :, k:k + 1], s.shape) for k in range(8)]
        for column, change_s, change_m in zip(columns, solved(rows_s), solved(rows_m)):
            s = s - column * change_s
            m = m - column * change_m
        work[rest] = pltpu.roll(s, n - 8, 2)
        unit[rest] = m

    for part in range(0, tiles, 4):
        pl.loop(part, part + 4)(functools.partial(step, rest=slice(part, tiles)))

    upper[...] = jnp.where(lane >= row, upper[...], 0.0)
    inverse[...] = jnp.where(lane <= row, inverse[...], 0.0)


def factor_kernel(ids_ref, mine_ref, other_ref, parts_ref, trailing_ref, r_ref, inv_ref, low_ref, copy_ref,
                  work, unit, upper, inverse, arrived):
    fetch = pltpu.make_async_copy(trailing_ref, copy_ref, arrived)
    fetch.start()
    tiled, flat = (HALF // 8, 8, HALF), (HALF, HALF)
    first = ids_ref[0] == 0
    for k in range(NX):
        rows = pl.ds(pl.multiple_of(64 * lax.rem(ids_ref[1] + NX - k, NX), 64), 64)
        mine, other = mine_ref[k], other_ref[k]
        r_ref[rows, :HALF] = jnp.where(first, mine, other)
        r_ref[rows, HALF:] = jnp.where(first, other, mine)
    right = r_ref[:, HALF:]
    work[...] = r_ref[:HALF, :HALF].reshape(tiled)
    eliminate(work, unit, upper, inverse)
    r_ref[:HALF, :HALF] = upper[...].reshape(flat)
    inverse_1 = inverse[...].reshape(flat)
    r_ref[HALF:, :HALF] = jnp.zeros(flat, F32)
    cross = dot(inverse_1, right[:HALF], precision=HIGHEST)
    r_ref[:HALF, HALF:] = cross
    work[...] = (right[HALF:] - dot(cross, cross, ((0,), (0,)), HIGHEST)).reshape(tiled)
    lower = dot(cross, inverse_1, ((0,), (0,)), HIGHEST)
    eliminate(work, unit, upper, inverse)
    r_ref[HALF:, HALF:] = upper[...].reshape(flat)
    inverse_2 = inverse[...].reshape(flat)
    below = -dot(inverse_2, lower, precision=HIGHEST)
    zero = jnp.zeros(flat, BF16)
    for start, one, two, three in zip((0, B), split(inverse_1, 2), split(below, 2), split(inverse_2, 2)):
        inv_ref[start:start + HALF, :HALF] = one
        inv_ref[start:start + HALF, HALF:] = zero
        inv_ref[start + HALF:start + B, :HALF] = two
        inv_ref[start + HALF:start + B, HALF:] = three
    basis = dot_split(inv_ref[...], parts_ref[:B], parts_ref[B:])
    low_ref[...] = basis.T.astype(BF16)
    fetch.wait()


def update_kernel(ids_ref, a0_ref, a1_ref, a2_ref, a3_ref, inv_ref, low_ref, trailing_ref, top_ref, updated_ref,
                  sums, top, updated, sent):
    for k, a_ref in enumerate((a0_ref, a1_ref, a2_ref, a3_ref)):
        sums[pl.ds(pl.multiple_of(64 * lax.rem(ids_ref[1] + NX - k, NX), 64), 64)] = a_ref[...]
    results = []

    def send(source, target, semaphore):
        results.append(pltpu.make_async_copy(source, target, semaphore))
        results[-1].start()

    for tile in range(0, COLS // TILE, WIDE):
        columns = slice(tile * TILE, (tile + WIDE) * TILE)
        rows = dot_split(inv_ref[...], *split(sums[:, columns], 2))
        top[:, columns] = rows
        send(top.at[:, columns], top_ref.at[:, columns], sent.at[0, tile])
        change = dot(low_ref[...], rows.astype(BF16))
        updated[:, columns] = (trailing_ref[:, columns].astype(F32) - change).astype(BF16)
        send(updated.at[:, columns], updated_ref.at[:, columns], sent.at[1, tile])
    for result in results:
        result.wait()


HBM = pl.BlockSpec(memory_space=pltpu.HBM)
VMEM = pl.BlockSpec(memory_space=pltpu.VMEM)
SMEM = pl.BlockSpec(memory_space=pltpu.SMEM)


def cost(flops, size):
    return pl.CostEstimate(flops=int(flops), bytes_accessed=int(size), transcendentals=0)


def limit(mib):
    return pltpu.CompilerParams(vmem_limit_bytes=mib * 2**20)


def array(*shape, dtype=F32):
    return jax.ShapeDtypeStruct(shape, dtype)


def product(ids, mine, other, trailing):
    return pl.pallas_call(
        product_kernel,
        out_shape=(array(2 * B, ROWS, dtype=BF16),) + (array(B // NX, COLS + HALF),) * NX,
        in_specs=[SMEM] + [VMEM] * 8 + [HBM],
        out_specs=(VMEM,) * (1 + NX),
        scratch_shapes=[
            pltpu.VMEM((ROWS, COLS), BF16),
            pltpu.VMEM((B, ROWS), BF16),
            pltpu.VMEM((2, B, 2 * TILE), F32),
            pltpu.VMEM((B, HALF), F32),
            pltpu.SemaphoreType.DMA((COLS // TILE,)),
        ],
        compiler_params=limit(50),
        cost_estimate=cost(3.6e9, 8e6),
    )(ids, *mine, *other, trailing)


def factor(ids, mine, other, parts, trailing):
    return pl.pallas_call(
        factor_kernel,
        out_shape=(
            array(B, B),
            array(2 * B, B, dtype=BF16),
            array(ROWS, B, dtype=BF16),
            array(ROWS, COLS, dtype=BF16),
        ),
        in_specs=[SMEM, VMEM, VMEM, VMEM, HBM],
        out_specs=(VMEM,) * 4,
        scratch_shapes=[pltpu.VMEM((HALF // 8, 8, HALF), F32)] * 4 + [pltpu.SemaphoreType.DMA],
        compiler_params=limit(45),
        cost_estimate=cost(3.5e9, 1e3),
    )(ids, mine, other, parts, trailing)


def update(ids, a, inverse, low, trailing):
    tiles = COLS // TILE
    return pl.pallas_call(
        update_kernel,
        out_shape=(array(B, COLS), array(ROWS, COLS, dtype=BF16)),
        in_specs=[SMEM] + [VMEM] * 7,
        out_specs=(HBM, HBM),
        scratch_shapes=[
            pltpu.VMEM((B, COLS), F32),
            pltpu.VMEM((B, COLS), F32),
            pltpu.VMEM((ROWS, COLS), BF16),
            pltpu.SemaphoreType.DMA((2, tiles)),
        ],
        compiler_params=limit(36),
        cost_estimate=cost(3e9, 12e6),
    )(ids, *a, inverse, low, trailing)


def add(pieces):
    count = 4 * (COLS + HALF) // HALF
    return pl.pallas_call(
        add_kernel,
        out_shape=(array(16, HALF),) * count,
        in_specs=[VMEM] * 4,
        out_specs=(VMEM,) * count,
        compiler_params=limit(16),
        cost_estimate=cost(1e6, 3e6),
    )(*pieces)


def join(blocks):
    return pl.pallas_call(
        join_kernel,
        out_shape=(array(64, COLS), array(64, HALF)),
        in_specs=[VMEM] * len(blocks),
        out_specs=(VMEM,) * 2,
        compiler_params=limit(16),
        cost_estimate=cost(1e6, 1e6),
    )(*blocks)


def shift(pieces, axis, routes):
    return [pieces[0]] + [lax.ppermute(pieces[k], axis, routes[k]) for k in range(1, 4)]


def local(panel, trailing):
    row, col = lax.axis_index("row"), lax.axis_index("col")
    ids = jnp.stack([col % 2, row // NZ, col // 2]).astype(jnp.int32)
    with jax.named_scope("gather_panel"):
        mine = shift([panel.T] * 4, "col", Y_ROUTES)
        other = [lax.ppermute(piece, "col", SIBLING) for piece in mine]
    with jax.named_scope("product"):
        parts, *pieces = product(ids, mine, other, trailing)
    with jax.named_scope("sum_x"):
        blocks = add(shift(pieces, "row", X_ROUTES))
    with jax.named_scope("sum_z"):
        sums, gram = join(lax.psum(tuple(blocks), "row", axis_index_groups=Z_GROUPS))
    with jax.named_scope("gather_gram"):
        gram_mine = jnp.stack(shift([gram] * NX, "row", X_ROUTES))
        gram_other = lax.ppermute(gram_mine, "col", SIBLING)
    with jax.named_scope("gather_x"):
        blocks = shift([sums] * NX, "row", X_ROUTES)
    with jax.named_scope("factor"):
        r_factor, inverse, low, trailing = factor(ids, gram_mine, gram_other, parts, trailing)
    with jax.named_scope("update"):
        top, updated = update(ids, blocks, inverse, low, trailing)
    return r_factor, top, updated


def solution(mesh):
    return jax.shard_map(
        local,
        mesh=mesh,
        in_specs=(P("row", "col"), P("row", "col")),
        out_specs=(P(), P(None, "col"), P("row", "col")),
        check_vma=False,
    )
```

```python
import functools

import jax
import jax.numpy as jnp
from jax import lax
from jax.experimental import pallas as pl
from jax.experimental.pallas import tpu as pltpu
from jax.sharding import PartitionSpec as P

F32 = jnp.float32
BF16 = jnp.bfloat16
HIGHEST = lax.Precision.HIGHEST
NX, NZ = 4, 8
B, ROWS, COLS, HALF, TILE = 256, 1024, 2048, 128, 256
WIDE = 4

Z_GROUPS = [[x * NZ + z for z in range(NZ)] for x in range(NX)]
SIBLING = [(c, c ^ 1) for c in range(8)]
Y_ROUTES = [[(c, (c + 2 * k) % 8) for c in range(8)] for k in range(4)]
X_ROUTES = [[(x * NZ + z, (x + k) % NX * NZ + z) for x in range(NX) for z in range(NZ)] for k in range(NX)]


def dot(a, b, contract=((1,), (0,)), precision=None):
    return lax.dot_general(a, b, (contract, ((), ())), precision=precision, preferred_element_type=F32)


def split(value, count):
    terms = []
    for _ in range(count):
        terms.append(value.astype(BF16))
        value = value - terms[-1].astype(F32)
    return terms


def dot_split(left, high, low):
    rows = left.shape[0] // 2
    both = dot(left, high)
    return both[rows:] + dot(left[:rows], low) + both[:rows]


def tile_of(index):
    return slice(index * TILE, index * TILE + TILE)


def fetches(source_ref, target_ref, arrived):
    copies = [
        pltpu.make_async_copy(source_ref.at[:, tile_of(tile)], target_ref.at[:, tile_of(tile)], arrived.at[tile])
        for tile in range(COLS // TILE)
    ]
    for copy in copies:
        copy.start()
    return copies


def product_kernel(ids_ref, *refs):
    mine, other, trailing_ref, parts_ref, pieces = refs[:4], refs[4:8], refs[8], refs[9], refs[10:10 + NX]
    held, third, whole, gram, arrived = refs[10 + NX:]
    copies = fetches(trailing_ref, held, arrived)
    core, x, y = ids_ref[0], ids_ref[1], ids_ref[2]
    for k in range(4):
        for ref, offset in ((mine[k], 32 * core), (other[k], 32 - 32 * core)):
            start = 64 * lax.rem(y + 4 - k, 4) + offset
            high, middle, low = split(ref[...], 3)
            parts_ref[pl.ds(pl.multiple_of(start, 32), 32)] = high
            parts_ref[pl.ds(pl.multiple_of(B + start, 32), 32)] = middle
            third[pl.ds(pl.multiple_of(start, 32), 32)] = low
    half = pl.multiple_of(core * HALF, HALF)
    last = ((1,), (1,))
    one = dot(parts_ref[...], parts_ref[pl.ds(half, HALF)], last)
    two = dot(parts_ref[...], parts_ref[pl.ds(pl.multiple_of(B + half, HALF), HALF)], last)
    small = dot(third[...], parts_ref[pl.ds(half, HALF)], last) + dot(parts_ref[:B], third[pl.ds(half, HALF)], last)
    gram[...] = small + two[B:] + one[B:] + two[:B] + one[:B]

    def hand_out(source, columns):
        for k in range(NX):
            start = pl.multiple_of(64 * lax.rem(x + k, NX), 64)
            pieces[k][:, columns] = source[pl.ds(start, 64)]

    hand_out(gram, slice(COLS, COLS + HALF))
    for tile in range(0, COLS // TILE, 2):
        for copy in copies[tile:tile + 2]:
            copy.wait()
        columns = slice(tile * TILE, (tile + 2) * TILE)
        both = dot(parts_ref[...], held[:, columns])
        slot = whole.at[tile // 2 % 2]
        slot[...] = both[B:] + both[:B]
        hand_out(slot, columns)


def bring_kernel(source_ref, target_ref, arrived):
    fetch = pltpu.make_async_copy(source_ref, target_ref, arrived)
    fetch.start()
    fetch.wait()


def blocks_of(ref):
    return [(slice(r, r + 16), slice(c, c + HALF)) for r in range(0, 64, 16) for c in range(0, ref.shape[1], HALF)]


def add_kernel(p0_ref, p1_ref, p2_ref, p3_ref, *outs):
    for out, place in zip(outs, blocks_of(p0_ref)):
        out[...] = p0_ref[place] + p1_ref[place] + (p2_ref[place] + p3_ref[place])


def join_kernel(*refs):
    blocks, sums_ref, gram_ref = refs[:-2], refs[-2], refs[-1]
    count = (COLS + HALF) // HALF
    for at, block in enumerate(blocks):
        row, column = divmod(at, count)
        rows = slice(16 * row, 16 * row + 16)
        if column < count - 1:
            sums_ref[rows, column * HALF:column * HALF + HALF] = block[...]
        else:
            gram_ref[rows] = block[...]


def eliminate(work, unit, upper, inverse):
    n, tiles = HALF, HALF // 8
    shape = (tiles, 8, n)
    row = 8 * lax.broadcasted_iota(jnp.int32, shape, 0) + lax.broadcasted_iota(jnp.int32, shape, 1)
    lane = lax.broadcasted_iota(jnp.int32, shape, 2)
    eight = lax.broadcasted_iota(jnp.int32, (8, n), 0)
    unit[...] = (lane == row).astype(F32)

    def reciprocal_root(value):
        guess = lax.rsqrt(value)
        return guess * (1.5 - 0.5 * value * guess * guess)

    def total(terms):
        while len(terms) > 1:
            terms = [sum(terms[at:at + 2]) for at in range(0, len(terms), 2)]
        return terms[0]

    def step(block, rest):
        pivot_s, pivot_m = work[block], unit[block]
        rows_s = [jnp.broadcast_to(pivot_s[k:k + 1], (8, n)) for k in range(8)]
        rows_m = [jnp.broadcast_to(pivot_m[k:k + 1], (8, n)) for k in range(8)]
        value = {(i, k): jnp.broadcast_to(pivot_s[i:i + 1, k:k + 1], (8, n)) for i in range(8) for k in range(i + 1)}
        low, inv = {}, {}
        for k in range(8):
            root = reciprocal_root(value[k, k])
            for i in range(k + 1, 8):
                low[i, k] = value[i, k] * root
            for i in range(k + 1, 8):
                for q in range(k + 1, i + 1):
                    value[i, q] = value[i, q] - low[i, k] * low[q, k]
            inv[k, k] = root
            for q in range(k):
                inv[k, q] = -root * total([low[k, t] * inv[t, q] for t in range(q, k)])

        def scaled(items):
            return [total([inv[i, k] * items[k] for k in range(i + 1)]) for i in range(8)]

        def solved(items):
            return [total([inv[i, k] * items[i] for i in range(k, 8)]) for k in range(8)]

        rows_s, rows_m = scaled(rows_s), scaled(rows_m)
        done_s, done_m = rows_s[0], rows_m[0]
        for k in range(1, 8):
            done_s = jnp.where(eight == k, rows_s[k], done_s)
            done_m = jnp.where(eight == k, rows_m[k], done_m)
        upper[block] = pltpu.roll(done_s, 8 * block, 1)
        inverse[block] = done_m
        s, m = work[rest], unit[rest]
        columns = [jnp.broadcast_to(s[:, :, k:k + 1], s.shape) for k in range(8)]
        for column, change_s, change_m in zip(columns, solved(rows_s), solved(rows_m)):
            s = s - column * change_s
            m = m - column * change_m
        work[rest] = pltpu.roll(s, n - 8, 2)
        unit[rest] = m

    for part in range(0, tiles, 4):
        pl.loop(part, part + 4)(functools.partial(step, rest=slice(part, tiles)))

    upper[...] = jnp.where(lane >= row, upper[...], 0.0)
    inverse[...] = jnp.where(lane <= row, inverse[...], 0.0)


def factor_kernel(ids_ref, mine_ref, other_ref, parts_ref, trailing_ref, r_ref, inv_ref, low_ref, copy_ref,
                  work, unit, upper, inverse, arrived):
    fetch = pltpu.make_async_copy(trailing_ref, copy_ref, arrived)
    fetch.start()
    tiled, flat = (HALF // 8, 8, HALF), (HALF, HALF)
    first = ids_ref[0] == 0
    for k in range(NX):
        rows = pl.ds(pl.multiple_of(64 * lax.rem(ids_ref[1] + NX - k, NX), 64), 64)
        mine, other = mine_ref[k], other_ref[k]
        r_ref[rows, :HALF] = jnp.where(first, mine, other)
        r_ref[rows, HALF:] = jnp.where(first, other, mine)
    right = r_ref[:, HALF:]
    work[...] = r_ref[:HALF, :HALF].reshape(tiled)
    eliminate(work, unit, upper, inverse)
    r_ref[:HALF, :HALF] = upper[...].reshape(flat)
    inverse_1 = inverse[...].reshape(flat)
    r_ref[HALF:, :HALF] = jnp.zeros(flat, F32)
    cross = dot(inverse_1, right[:HALF], precision=HIGHEST)
    r_ref[:HALF, HALF:] = cross
    work[...] = (right[HALF:] - dot(cross, cross, ((0,), (0,)), HIGHEST)).reshape(tiled)
    lower = dot(cross, inverse_1, ((0,), (0,)), HIGHEST)
    eliminate(work, unit, upper, inverse)
    r_ref[HALF:, HALF:] = upper[...].reshape(flat)
    inverse_2 = inverse[...].reshape(flat)
    below = -dot(inverse_2, lower, precision=HIGHEST)
    zero = jnp.zeros(flat, BF16)
    for start, one, two, three in zip((0, B), split(inverse_1, 2), split(below, 2), split(inverse_2, 2)):
        inv_ref[start:start + HALF, :HALF] = one
        inv_ref[start:start + HALF, HALF:] = zero
        inv_ref[start + HALF:start + B, :HALF] = two
        inv_ref[start + HALF:start + B, HALF:] = three
    basis = dot_split(inv_ref[...], parts_ref[:B], parts_ref[B:])
    low_ref[...] = basis.T.astype(BF16)
    fetch.wait()


def update_kernel(ids_ref, a0_ref, a1_ref, a2_ref, a3_ref, inv_ref, low_ref, trailing_ref, top_ref, updated_ref,
                  sums, top, updated, sent):
    for k, a_ref in enumerate((a0_ref, a1_ref, a2_ref, a3_ref)):
        sums[pl.ds(pl.multiple_of(64 * lax.rem(ids_ref[1] + NX - k, NX), 64), 64)] = a_ref[...]
    results = []

    def send(source, target, semaphore):
        results.append(pltpu.make_async_copy(source, target, semaphore))
        results[-1].start()

    for tile in range(0, COLS // TILE, WIDE):
        columns = slice(tile * TILE, (tile + WIDE) * TILE)
        rows = dot_split(inv_ref[...], *split(sums[:, columns], 2))
        top[:, columns] = rows
        send(top.at[:, columns], top_ref.at[:, columns], sent.at[0, tile])
        change = dot(low_ref[...], rows.astype(BF16))
        updated[:, columns] = (trailing_ref[:, columns].astype(F32) - change).astype(BF16)
        send(updated.at[:, columns], updated_ref.at[:, columns], sent.at[1, tile])
    for result in results:
        result.wait()


HBM = pl.BlockSpec(memory_space=pltpu.HBM)
VMEM = pl.BlockSpec(memory_space=pltpu.VMEM)
SMEM = pl.BlockSpec(memory_space=pltpu.SMEM)


def cost(flops, size):
    return pl.CostEstimate(flops=int(flops), bytes_accessed=int(size), transcendentals=0)


def limit(mib):
    return pltpu.CompilerParams(vmem_limit_bytes=mib * 2**20)


def array(*shape, dtype=F32):
    return jax.ShapeDtypeStruct(shape, dtype)


def product(ids, mine, other, trailing):
    return pl.pallas_call(
        product_kernel,
        out_shape=(array(2 * B, ROWS, dtype=BF16),) + (array(B // NX, COLS + HALF),) * NX,
        in_specs=[SMEM] + [VMEM] * 8 + [HBM],
        out_specs=(VMEM,) * (1 + NX),
        scratch_shapes=[
            pltpu.VMEM((ROWS, COLS), BF16),
            pltpu.VMEM((B, ROWS), BF16),
            pltpu.VMEM((2, B, 2 * TILE), F32),
            pltpu.VMEM((B, HALF), F32),
            pltpu.SemaphoreType.DMA((COLS // TILE,)),
        ],
        compiler_params=limit(50),
        cost_estimate=cost(3.6e9, 8e6),
    )(ids, *mine, *other, trailing)


def factor(ids, mine, other, parts, trailing):
    return pl.pallas_call(
        factor_kernel,
        out_shape=(
            array(B, B),
            array(2 * B, B, dtype=BF16),
            array(ROWS, B, dtype=BF16),
            array(ROWS, COLS, dtype=BF16),
        ),
        in_specs=[SMEM, VMEM, VMEM, VMEM, HBM],
        out_specs=(VMEM,) * 4,
        scratch_shapes=[pltpu.VMEM((HALF // 8, 8, HALF), F32)] * 4 + [pltpu.SemaphoreType.DMA],
        compiler_params=limit(45),
        cost_estimate=cost(3.5e9, 1e3),
    )(ids, mine, other, parts, trailing)


def update(ids, a, inverse, low, trailing):
    tiles = COLS // TILE
    return pl.pallas_call(
        update_kernel,
        out_shape=(array(B, COLS), array(ROWS, COLS, dtype=BF16)),
        in_specs=[SMEM] + [VMEM] * 7,
        out_specs=(HBM, HBM),
        scratch_shapes=[
            pltpu.VMEM((B, COLS), F32),
            pltpu.VMEM((B, COLS), F32),
            pltpu.VMEM((ROWS, COLS), BF16),
            pltpu.SemaphoreType.DMA((2, tiles)),
        ],
        compiler_params=limit(36),
        cost_estimate=cost(3e9, 12e6),
    )(ids, *a, inverse, low, trailing)


def add(pieces):
    count = 4 * (COLS + HALF) // HALF
    return pl.pallas_call(
        add_kernel,
        out_shape=(array(16, HALF),) * count,
        in_specs=[VMEM] * 4,
        out_specs=(VMEM,) * count,
        compiler_params=limit(16),
        cost_estimate=cost(1e6, 3e6),
    )(*pieces)


def join(blocks):
    return pl.pallas_call(
        join_kernel,
        out_shape=(array(64, COLS), array(64, HALF)),
        in_specs=[VMEM] * len(blocks),
        out_specs=(VMEM,) * 2,
        compiler_params=limit(16),
        cost_estimate=cost(1e6, 1e6),
    )(*blocks)


def bring(value):
    return pl.pallas_call(
        bring_kernel,
        out_shape=array(*value.shape, dtype=value.dtype),
        in_specs=[HBM],
        out_specs=VMEM,
        scratch_shapes=[pltpu.SemaphoreType.DMA],
        compiler_params=limit(45),
        cost_estimate=cost(1e6, 2e6),
    )(value)


def shift(pieces, axis, routes):
    return [pieces[0]] + [lax.ppermute(pieces[k], axis, routes[k]) for k in range(1, 4)]


def local(panel, trailing):
    row, col = lax.axis_index("row"), lax.axis_index("col")
    ids = jnp.stack([col % 2, row // NZ, col // 2]).astype(jnp.int32)
    with jax.named_scope("gather_panel"):
        mine = shift([panel.T] * 4, "col", Y_ROUTES)
        other = [lax.ppermute(piece, "col", SIBLING) for piece in mine]
        mine[0] = bring(mine[0])
    with jax.named_scope("product"):
        parts, *pieces = product(ids, mine, other, trailing)
    with jax.named_scope("sum_x"):
        blocks = add(shift(pieces, "row", X_ROUTES))
    with jax.named_scope("sum_z"):
        sums, gram = join(lax.psum(tuple(blocks), "row", axis_index_groups=Z_GROUPS))
    with jax.named_scope("gather_gram"):
        gram_mine = jnp.stack(shift([gram] * NX, "row", X_ROUTES))
        gram_other = lax.ppermute(gram_mine, "col", SIBLING)
    with jax.named_scope("gather_x"):
        blocks = shift([sums] * NX, "row", X_ROUTES)
    with jax.named_scope("factor"):
        r_factor, inverse, low, trailing = factor(ids, gram_mine, gram_other, parts, trailing)
    with jax.named_scope("update"):
        top, updated = update(ids, blocks, inverse, low, trailing)
    return r_factor, top, updated


def solution(mesh):
    return jax.shard_map(
        local,
        mesh=mesh,
        in_specs=(P("row", "col"), P("row", "col")),
        out_specs=(P(), P(None, "col"), P("row", "col")),
        check_vma=False,
    )
```

```python
import functools

import jax
import jax.numpy as jnp
from jax import lax
from jax.experimental import pallas as pl
from jax.experimental.pallas import tpu as pltpu
from jax.sharding import PartitionSpec as P

F32 = jnp.float32
BF16 = jnp.bfloat16
HIGHEST = lax.Precision.HIGHEST
NX, NZ = 4, 8
B, ROWS, COLS, HALF, TILE = 256, 1024, 2048, 128, 256
WIDE = 2

Z_GROUPS = [[x * NZ + z for z in range(NZ)] for x in range(NX)]
SIBLING = [(c, c ^ 1) for c in range(8)]
Y_ROUTES = [[(c, (c + 2 * k) % 8) for c in range(8)] for k in range(4)]
X_ROUTES = [[(x * NZ + z, (x + k) % NX * NZ + z) for x in range(NX) for z in range(NZ)] for k in range(NX)]


def dot(a, b, contract=((1,), (0,)), precision=None):
    return lax.dot_general(a, b, (contract, ((), ())), precision=precision, preferred_element_type=F32)


def split(value, count):
    terms = []
    for _ in range(count):
        terms.append(value.astype(BF16))
        value = value - terms[-1].astype(F32)
    return terms


def dot_split(left, high, low):
    rows = left.shape[0] // 2
    both = dot(left, high)
    return both[rows:] + dot(left[:rows], low) + both[:rows]


def tile_of(index):
    return slice(index * TILE, index * TILE + TILE)


def fetches(source_ref, target_ref, arrived):
    copies = [
        pltpu.make_async_copy(source_ref.at[:, tile_of(tile)], target_ref.at[:, tile_of(tile)], arrived.at[tile])
        for tile in range(COLS // TILE)
    ]
    for copy in copies:
        copy.start()
    return copies


def product_kernel(ids_ref, *refs):
    mine, other, trailing_ref, parts_ref, pieces = refs[:4], refs[4:8], refs[8], refs[9], refs[10:10 + NX]
    held, third, whole, gram, arrived = refs[10 + NX:]
    copies = fetches(trailing_ref, held, arrived)
    core, x, y = ids_ref[0], ids_ref[1], ids_ref[2]
    for k in range(4):
        for ref, offset in ((mine[k], 32 * core), (other[k], 32 - 32 * core)):
            start = 64 * lax.rem(y + 4 - k, 4) + offset
            high, middle, low = split(ref[...], 3)
            parts_ref[pl.ds(pl.multiple_of(start, 32), 32)] = high
            parts_ref[pl.ds(pl.multiple_of(B + start, 32), 32)] = middle
            third[pl.ds(pl.multiple_of(start, 32), 32)] = low
    half = pl.multiple_of(core * HALF, HALF)
    last = ((1,), (1,))
    one = dot(parts_ref[...], parts_ref[pl.ds(half, HALF)], last)
    two = dot(parts_ref[...], parts_ref[pl.ds(pl.multiple_of(B + half, HALF), HALF)], last)
    small = dot(third[...], parts_ref[pl.ds(half, HALF)], last) + dot(parts_ref[:B], third[pl.ds(half, HALF)], last)
    gram[...] = small + two[B:] + one[B:] + two[:B] + one[:B]

    def hand_out(source, columns):
        for k in range(NX):
            start = pl.multiple_of(64 * lax.rem(x + k, NX), 64)
            pieces[k][:, columns] = source[pl.ds(start, 64)]

    hand_out(gram, slice(COLS, COLS + HALF))
    for tile in range(0, COLS // TILE, 2):
        for copy in copies[tile:tile + 2]:
            copy.wait()
        columns = slice(tile * TILE, (tile + 2) * TILE)
        both = dot(parts_ref[...], held[:, columns])
        slot = whole.at[tile // 2 % 2]
        slot[...] = both[B:] + both[:B]
        hand_out(slot, columns)


def bring_kernel(source_ref, target_ref, arrived):
    fetch = pltpu.make_async_copy(source_ref, target_ref, arrived)
    fetch.start()
    fetch.wait()


def blocks_of(ref):
    return [(slice(r, r + 16), slice(c, c + HALF)) for r in range(0, 64, 16) for c in range(0, ref.shape[1], HALF)]


def add_kernel(p0_ref, p1_ref, p2_ref, p3_ref, *outs):
    for out, place in zip(outs, blocks_of(p0_ref)):
        out[...] = p0_ref[place] + p1_ref[place] + (p2_ref[place] + p3_ref[place])


def join_kernel(*refs):
    blocks, sums_ref, gram_ref = refs[:-2], refs[-2], refs[-1]
    count = (COLS + HALF) // HALF
    for at, block in enumerate(blocks):
        row, column = divmod(at, count)
        rows = slice(16 * row, 16 * row + 16)
        if column < count - 1:
            sums_ref[rows, column * HALF:column * HALF + HALF] = block[...]
        else:
            gram_ref[rows] = block[...]


def eliminate(work, unit, upper, inverse):
    n, tiles = HALF, HALF // 8
    shape = (tiles, 8, n)
    row = 8 * lax.broadcasted_iota(jnp.int32, shape, 0) + lax.broadcasted_iota(jnp.int32, shape, 1)
    lane = lax.broadcasted_iota(jnp.int32, shape, 2)
    eight = lax.broadcasted_iota(jnp.int32, (8, n), 0)
    unit[...] = (lane == row).astype(F32)

    def reciprocal_root(value):
        guess = lax.rsqrt(value)
        return guess * (1.5 - 0.5 * value * guess * guess)

    def total(terms):
        while len(terms) > 1:
            terms = [sum(terms[at:at + 2]) for at in range(0, len(terms), 2)]
        return terms[0]

    def step(block, rest):
        pivot_s, pivot_m = work[block], unit[block]
        rows_s = [jnp.broadcast_to(pivot_s[k:k + 1], (8, n)) for k in range(8)]
        rows_m = [jnp.broadcast_to(pivot_m[k:k + 1], (8, n)) for k in range(8)]
        value = {(i, k): jnp.broadcast_to(pivot_s[i:i + 1, k:k + 1], (8, n)) for i in range(8) for k in range(i + 1)}
        low, inv = {}, {}
        for k in range(8):
            root = reciprocal_root(value[k, k])
            for i in range(k + 1, 8):
                low[i, k] = value[i, k] * root
            for i in range(k + 1, 8):
                for q in range(k + 1, i + 1):
                    value[i, q] = value[i, q] - low[i, k] * low[q, k]
            inv[k, k] = root
            for q in range(k):
                inv[k, q] = -root * total([low[k, t] * inv[t, q] for t in range(q, k)])

        def scaled(items):
            return [total([inv[i, k] * items[k] for k in range(i + 1)]) for i in range(8)]

        def solved(items):
            return [total([inv[i, k] * items[i] for i in range(k, 8)]) for k in range(8)]

        rows_s, rows_m = scaled(rows_s), scaled(rows_m)
        done_s, done_m = rows_s[0], rows_m[0]
        for k in range(1, 8):
            done_s = jnp.where(eight == k, rows_s[k], done_s)
            done_m = jnp.where(eight == k, rows_m[k], done_m)
        upper[block] = pltpu.roll(done_s, 8 * block, 1)
        inverse[block] = done_m
        s, m = work[rest], unit[rest]
        columns = [jnp.broadcast_to(s[:, :, k:k + 1], s.shape) for k in range(8)]
        for column, change_s, change_m in zip(columns, solved(rows_s), solved(rows_m)):
            s = s - column * change_s
            m = m - column * change_m
        work[rest] = pltpu.roll(s, n - 8, 2)
        unit[rest] = m

    for part in range(0, tiles, 4):
        pl.loop(part, part + 4)(functools.partial(step, rest=slice(part, tiles)))

    upper[...] = jnp.where(lane >= row, upper[...], 0.0)
    inverse[...] = jnp.where(lane <= row, inverse[...], 0.0)


def factor_kernel(ids_ref, mine_ref, other_ref, parts_ref, trailing_ref, r_ref, inv_ref, low_ref, copy_ref,
                  work, unit, upper, inverse, arrived):
    fetch = pltpu.make_async_copy(trailing_ref, copy_ref, arrived)
    fetch.start()
    tiled, flat = (HALF // 8, 8, HALF), (HALF, HALF)
    first = ids_ref[0] == 0
    for k in range(NX):
        rows = pl.ds(pl.multiple_of(64 * lax.rem(ids_ref[1] + NX - k, NX), 64), 64)
        mine, other = mine_ref[k], other_ref[k]
        r_ref[rows, :HALF] = jnp.where(first, mine, other)
        r_ref[rows, HALF:] = jnp.where(first, other, mine)
    right = r_ref[:, HALF:]
    work[...] = r_ref[:HALF, :HALF].reshape(tiled)
    eliminate(work, unit, upper, inverse)
    r_ref[:HALF, :HALF] = upper[...].reshape(flat)
    inverse_1 = inverse[...].reshape(flat)
    r_ref[HALF:, :HALF] = jnp.zeros(flat, F32)
    cross = dot(inverse_1, right[:HALF], precision=HIGHEST)
    r_ref[:HALF, HALF:] = cross
    work[...] = (right[HALF:] - dot(cross, cross, ((0,), (0,)), HIGHEST)).reshape(tiled)
    lower = dot(cross, inverse_1, ((0,), (0,)), HIGHEST)
    eliminate(work, unit, upper, inverse)
    r_ref[HALF:, HALF:] = upper[...].reshape(flat)
    inverse_2 = inverse[...].reshape(flat)
    below = -dot(inverse_2, lower, precision=HIGHEST)
    zero = jnp.zeros(flat, BF16)
    for start, one, two, three in zip((0, B), split(inverse_1, 2), split(below, 2), split(inverse_2, 2)):
        inv_ref[start:start + HALF, :HALF] = one
        inv_ref[start:start + HALF, HALF:] = zero
        inv_ref[start + HALF:start + B, :HALF] = two
        inv_ref[start + HALF:start + B, HALF:] = three
    basis = dot_split(inv_ref[...], parts_ref[:B], parts_ref[B:])
    low_ref[...] = basis.T.astype(BF16)
    fetch.wait()


def update_kernel(ids_ref, a0_ref, a1_ref, a2_ref, a3_ref, inv_ref, low_ref, trailing_ref, top_ref, updated_ref,
                  sums, top, updated, sent):
    for k, a_ref in enumerate((a0_ref, a1_ref, a2_ref, a3_ref)):
        sums[pl.ds(pl.multiple_of(64 * lax.rem(ids_ref[1] + NX - k, NX), 64), 64)] = a_ref[...]
    results = []

    def send(source, target, semaphore):
        results.append(pltpu.make_async_copy(source, target, semaphore))
        results[-1].start()

    for tile in range(0, COLS // TILE, WIDE):
        columns = slice(tile * TILE, (tile + WIDE) * TILE)
        rows = dot_split(inv_ref[...], *split(sums[:, columns], 2))
        top[:, columns] = rows
        send(top.at[:, columns], top_ref.at[:, columns], sent.at[0, tile])
        change = dot(low_ref[...], rows.astype(BF16))
        updated[:, columns] = (trailing_ref[:, columns].astype(F32) - change).astype(BF16)
        send(updated.at[:, columns], updated_ref.at[:, columns], sent.at[1, tile])
    for result in results:
        result.wait()


HBM = pl.BlockSpec(memory_space=pltpu.HBM)
VMEM = pl.BlockSpec(memory_space=pltpu.VMEM)
SMEM = pl.BlockSpec(memory_space=pltpu.SMEM)


def cost(flops, size):
    return pl.CostEstimate(flops=int(flops), bytes_accessed=int(size), transcendentals=0)


def limit(mib):
    return pltpu.CompilerParams(vmem_limit_bytes=mib * 2**20)


def array(*shape, dtype=F32):
    return jax.ShapeDtypeStruct(shape, dtype)


def product(ids, mine, other, trailing):
    return pl.pallas_call(
        product_kernel,
        out_shape=(array(2 * B, ROWS, dtype=BF16),) + (array(B // NX, COLS + HALF),) * NX,
        in_specs=[SMEM] + [VMEM] * 8 + [HBM],
        out_specs=(VMEM,) * (1 + NX),
        scratch_shapes=[
            pltpu.VMEM((ROWS, COLS), BF16),
            pltpu.VMEM((B, ROWS), BF16),
            pltpu.VMEM((2, B, 2 * TILE), F32),
            pltpu.VMEM((B, HALF), F32),
            pltpu.SemaphoreType.DMA((COLS // TILE,)),
        ],
        compiler_params=limit(50),
        cost_estimate=cost(3.6e9, 8e6),
    )(ids, *mine, *other, trailing)


def factor(ids, mine, other, parts, trailing):
    return pl.pallas_call(
        factor_kernel,
        out_shape=(
            array(B, B),
            array(2 * B, B, dtype=BF16),
            array(ROWS, B, dtype=BF16),
            array(ROWS, COLS, dtype=BF16),
        ),
        in_specs=[SMEM, VMEM, VMEM, VMEM, HBM],
        out_specs=(VMEM,) * 4,
        scratch_shapes=[pltpu.VMEM((HALF // 8, 8, HALF), F32)] * 4 + [pltpu.SemaphoreType.DMA],
        compiler_params=limit(45),
        cost_estimate=cost(3.5e9, 1e3),
    )(ids, mine, other, parts, trailing)


def update(ids, a, inverse, low, trailing):
    tiles = COLS // TILE
    return pl.pallas_call(
        update_kernel,
        out_shape=(array(B, COLS), array(ROWS, COLS, dtype=BF16)),
        in_specs=[SMEM] + [VMEM] * 7,
        out_specs=(HBM, HBM),
        scratch_shapes=[
            pltpu.VMEM((B, COLS), F32),
            pltpu.VMEM((B, COLS), F32),
            pltpu.VMEM((ROWS, COLS), BF16),
            pltpu.SemaphoreType.DMA((2, tiles)),
        ],
        compiler_params=limit(36),
        cost_estimate=cost(3e9, 12e6),
    )(ids, *a, inverse, low, trailing)


def add(pieces):
    count = 4 * (COLS + HALF) // HALF
    return pl.pallas_call(
        add_kernel,
        out_shape=(array(16, HALF),) * count,
        in_specs=[VMEM] * 4,
        out_specs=(VMEM,) * count,
        compiler_params=limit(16),
        cost_estimate=cost(1e6, 3e6),
    )(*pieces)


def join(blocks):
    return pl.pallas_call(
        join_kernel,
        out_shape=(array(64, COLS), array(64, HALF)),
        in_specs=[VMEM] * len(blocks),
        out_specs=(VMEM,) * 2,
        compiler_params=limit(16),
        cost_estimate=cost(1e6, 1e6),
    )(*blocks)


def bring(value):
    return pl.pallas_call(
        bring_kernel,
        out_shape=array(*value.shape, dtype=value.dtype),
        in_specs=[HBM],
        out_specs=VMEM,
        scratch_shapes=[pltpu.SemaphoreType.DMA],
        compiler_params=limit(45),
        cost_estimate=cost(1e6, 2e6),
    )(value)


def shift(pieces, axis, routes):
    return [pieces[0]] + [lax.ppermute(pieces[k], axis, routes[k]) for k in range(1, 4)]


def local(panel, trailing):
    row, col = lax.axis_index("row"), lax.axis_index("col")
    ids = jnp.stack([col % 2, row // NZ, col // 2]).astype(jnp.int32)
    with jax.named_scope("gather_panel"):
        mine = shift([panel.T] * 4, "col", Y_ROUTES)
        other = [lax.ppermute(piece, "col", SIBLING) for piece in mine]
        mine[0] = bring(mine[0])
    with jax.named_scope("product"):
        parts, *pieces = product(ids, mine, other, trailing)
    with jax.named_scope("sum_x"):
        blocks = add(shift(pieces, "row", X_ROUTES))
    with jax.named_scope("sum_z"):
        sums, gram = join(lax.psum(tuple(blocks), "row", axis_index_groups=Z_GROUPS))
    with jax.named_scope("gather_gram"):
        gram_mine = jnp.stack(shift([gram] * NX, "row", X_ROUTES))
        gram_other = lax.ppermute(gram_mine, "col", SIBLING)
    with jax.named_scope("gather_x"):
        blocks = shift([sums] * NX, "row", X_ROUTES)
    with jax.named_scope("factor"):
        r_factor, inverse, low, trailing = factor(ids, gram_mine, gram_other, parts, trailing)
    with jax.named_scope("update"):
        top, updated = update(ids, blocks, inverse, low, trailing)
    return r_factor, top, updated


def solution(mesh):
    return jax.shard_map(
        local,
        mesh=mesh,
        in_specs=(P("row", "col"), P("row", "col")),
        out_specs=(P(), P(None, "col"), P("row", "col")),
        check_vma=False,
    )
```
